32 devices in a mesh: pb: 8 (over y, x, core), ka: 4 (over z).
Axes of the slice: x: 2, y: 2, z: 4, core: 2. Of those that a mesh axis runs over, the one named last changes fastest.
Arguments:
- query_features: bfloat16 [32, 192, 256], P('pb'), may hold values from -6 to 6
- key_features: bfloat16 [192, 32, 256], P(None, 'ka'), may hold values from -6 to 6
- pyramid_grad: bfloat16 [6144, 4, 2040], P('pb', 'ka'), may hold values from -26.127891 to 26.127891, as said below
- query_image: bfloat16 [32, 192, 256], P('pb', 'ka'), may hold values from -0.125 to 0.125
- key_image: bfloat16 [192, 32, 256], P('pb', 'ka'), may hold values from -0.125 to 0.125
- conv_weight: bfloat16 [3, 3, 256, 256], replicated, may hold values from -0.125 to 0.125
Outputs:
- query_image_grad: bfloat16 [32, 192, 256], P('pb', 'ka')
- key_image_grad: bfloat16 [192, 32, 256], P('pb', 'ka')
- weight_grad: float32 [3, 3, 256, 256], replicated
The draws below stay inside these ranges and needn't reach their ends.
Inputs may be any that keep to these rules, and one draw needn't show every extreme that they name: pyramid_grad[q, k] holds the four levels of key strip k one after another as described in the reference program.
All inputs are finite; a program needn't handle non-finite values.
Results may differ from the reference program's by a relative error of at most 0.0056.
Values may be sent and summed in bfloat16 or wider, within the bound.
No kernel may reach another device: no remote copies, remote signals or barrier semaphores. Data moves between devices by JAX's collectives and lax.ppermute only.
A program may use at most 128 MiB of HBM per device.

```python
import math
import jax
import jax.numpy as jnp
from jax import lax

D = 256
CIN = 256
LEVELS = 4
W = 192
H = 32
KPACK = 2040
N_PB = 8
N_KA = 4


def draw_pyramid_grad(key, part):
    key_noise = jax.random.fold_in(key, 11)
    fine_count = N_PB * W
    position = jnp.arange(KPACK)
    tier = jnp.where(position >= fine_count, 1.0, 0.0)
    tier = tier + jnp.where(position >= fine_count + fine_count // 4, 1.0, 0.0)
    tier = tier + jnp.where(position >= fine_count + fine_count // 4 + fine_count // 16, 1.0, 0.0)
    tier_scale = 4.0 ** tier * (8.0 / math.sqrt(H * W))
    normal_part = jnp.clip(jax.random.normal(key_noise, (H * W, N_KA, KPACK), jnp.float32), -4.0, 4.0)
    return (normal_part * tier_scale).astype(jnp.bfloat16)


def shard_levels(key, extent, split, low, high):
    gain = 1.0
    for dim, blocks in split:
        draws = jax.random.uniform(jax.random.fold_in(jax.random.fold_in(key, 6), dim), (blocks,), jnp.float32, low / len(split), high / len(split))
        gain = gain * jnp.repeat(jnp.exp(draws), extent[dim] // blocks).reshape((-1,) + (1,) * (len(extent) - 1 - dim))
    return gain


def centred(rng, shape, scale, reach, split=(), held_as=jnp.bfloat16):
    array = scale * jax.random.normal(rng, shape, jnp.float32)
    if split:
        array = array * shard_levels(rng, shape, split, -0.22, 0.18)
    return jnp.clip(array, -reach, reach).astype(held_as)


def setup_inputs(seed: int = 0) -> dict:
    seeds = jax.random.split(jax.random.key(seed), 7)
    return {
        "query_features": centred(seeds[0], (H, W, D), 1.0, 6.0, ((0, 8),)),
        "key_features": centred(seeds[1], (W, H, D), 1.0, 6.0, ((1, 4),)),
        "pyramid_grad": draw_pyramid_grad(jax.random.fold_in(seeds[6], 71), 0),
        "query_image": centred(seeds[3], (H, W, CIN), ((2 * H * W) ** -0.5), 0.125, ((0, 8), (1, 4))),
        "key_image": centred(seeds[4], (W, H, CIN), ((2 * H * W) ** -0.5), 0.125, ((0, 8), (1, 4))),
        "conv_weight": centred(seeds[5], (3, 3, CIN, D), (9 * CIN) ** -0.5, 0.125),
    }


def pool_levels(strip):
    strip_float = strip.astype(jnp.float32)
    result = []
    for level_index in range(LEVELS):
        factor = 2 ** level_index
        cell_cols, key_rows, channels = strip_float.shape
        pooled = strip_float.reshape(cell_cols // factor, factor, key_rows // factor, factor, channels).mean(axis=(1, 3))
        result.append(pooled.astype(jnp.bfloat16))
    return result


def conv_backward(conv_input, padded_input, padded_grad, kernel):
    tile_rows = padded_grad.shape[0] - 2
    tile_cols = padded_grad.shape[1] - 2
    out_channels = padded_grad.shape[2]
    in_channels = kernel.shape[2]
    interior = padded_grad[1:1 + tile_rows, 1:1 + tile_cols].reshape(-1, out_channels)
    input_acc = jnp.zeros((tile_rows * tile_cols, in_channels), jnp.float32)
    kernel_rows = []
    for row_shift in range(3):
        kernel_row = []
        for col_shift in range(3):
            shifted = padded_grad[2 - row_shift:2 - row_shift + tile_rows, 2 - col_shift:2 - col_shift + tile_cols].reshape(-1, out_channels)
            input_acc = input_acc + lax.dot_general(shifted, kernel[row_shift, col_shift], (((1,), (1,)), ((), ())), preferred_element_type=jnp.float32)
            window = padded_input[row_shift:row_shift + tile_rows, col_shift:col_shift + tile_cols].reshape(-1, in_channels)
            weight_term = lax.dot_general(window, interior, (((0,), (0,)), ((), ())), preferred_element_type=jnp.float32)
            kernel_row.append(weight_term)
        kernel_rows.append(jnp.stack(kernel_row))
    return input_acc.reshape(tile_rows, tile_cols, in_channels), jnp.stack(kernel_rows)


def reference(query_features, key_features, pyramid_grad, query_image, key_image, conv_weight):
    norm_scale = D ** -0.5
    height, width_cells, channels = query_features.shape
    queries = query_features.reshape(height * width_cells, channels)
    key_rows = height // N_KA
    query_acc = jnp.zeros((height * width_cells, channels), jnp.float32)
    strip_list = []
    for strip_index in range(N_KA):
        strip = key_features[:, strip_index * key_rows:(strip_index + 1) * key_rows, :]
        pooled = pool_levels(strip)
        strip_grads = pyramid_grad[:, strip_index, :]
        key_acc = jnp.zeros((width_cells, key_rows, channels), jnp.float32)
        offset = 0
        for level_index in range(LEVELS):
            factor = 2 ** level_index
            grid_rows = key_rows // factor
            grid_cols = width_cells // factor
            cell_count = grid_rows * grid_cols
            grad_block = strip_grads[:, offset:offset + cell_count]
            offset = offset + cell_count
            ordered = jnp.transpose(pooled[level_index], (1, 0, 2)).reshape(cell_count, channels)
            query_acc = query_acc + jnp.dot(grad_block, ordered, preferred_element_type=jnp.float32)
            coarse = lax.dot_general(grad_block, queries, (((0,), (0,)), ((), ())), preferred_element_type=jnp.float32)
            coarse = jnp.transpose(coarse.reshape(grid_rows, grid_cols, channels), (1, 0, 2))
            spread = jnp.broadcast_to(coarse[:, None, :, None, :], (grid_cols, factor, grid_rows, factor, channels)).reshape(width_cells, key_rows, channels)
            key_acc = key_acc + spread / (4.0 ** level_index)
        strip_list.append(key_acc)
    query_grad = (query_acc * norm_scale).reshape(height, width_cells, channels).astype(jnp.bfloat16)
    key_grad = (jnp.concatenate(strip_list, axis=1) * norm_scale).astype(jnp.bfloat16)
    pad_spec = ((1, 1), (1, 1), (0, 0))
    grad_first, weight_first = conv_backward(query_image, jnp.pad(query_image, pad_spec), jnp.pad(query_grad, pad_spec), conv_weight)
    image_second = jnp.transpose(key_image, (1, 0, 2))
    grad_rows = jnp.transpose(key_grad, (1, 0, 2))
    grad_second, weight_second = conv_backward(image_second, jnp.pad(image_second, pad_spec), jnp.pad(grad_rows, pad_spec), conv_weight)
    query_image_grad = grad_first.astype(jnp.bfloat16)
    key_image_grad = jnp.transpose(grad_second, (1, 0, 2)).astype(jnp.bfloat16)
    return query_image_grad, key_image_grad, weight_first + weight_second
```

```python
import functools

import jax
import jax.numpy as jnp
from jax import lax
from jax.experimental import pallas as pl
from jax.experimental.pallas import tpu as pltpu
from jax.sharding import PartitionSpec as P

LEVELS = 4
F32 = jnp.float32
BF16 = jnp.bfloat16
VMEM_BYTES = 56 * 2**20


def flip(count, mask):
    return [(i, i ^ mask) for i in range(count)]


def ordered(parts, index):
    count = len(parts)
    bit = 1
    while bit < count:
        swap = (index & bit) != 0
        parts = [jnp.where(swap, parts[a ^ bit], parts[a]) for a in range(count)]
        bit *= 2
    return parts


def pick(blocks, index):
    return lax.dynamic_index_in_dim(blocks, index, 0, keepdims=False)


def put(ref, rows, value):
    for lane in range(ref.shape[0]):
        ref[lane, rows, :] = value[:, lane * 128 : (lane + 1) * 128]


def get(ref, rows):
    return jnp.concatenate([ref[lane, rows, :] for lane in range(ref.shape[0])], axis=1)


def corr_kernel(width, key_rows, tile_q, tile_k, n_ka, n_quad, a_ref, q_ref, key_ref, *rest):
    q_outs = rest[:n_ka]
    send_ref, keep_ref, cells_ref, cells16_ref, coarse_ref, keyf_ref, tmp_ref, kpad_ref, qpad_ref, stage_ref = rest[n_ka:]
    step = pl.program_id(0)
    steps = pl.num_programs(0)
    channels = q_ref.shape[1]
    scale = channels ** (-0.5)
    z = lax.axis_index("ka")
    pb = lax.axis_index("pb")
    core = pb % 2
    quad = pb // 2

    @pl.when(step == 0)
    def _():
        put(keyf_ref, slice(None), key_ref[...].astype(F32))
        rows = [get(keyf_ref, pl.ds(r, width, stride=key_rows)) for r in range(key_rows)]
        offset = 0
        for level in range(LEVELS):
            w = width >> level
            if level:
                pairs = []
                for i in range(len(rows) // 2):
                    put(tmp_ref, slice(0, 2 * w), rows[2 * i] + rows[2 * i + 1])
                    pairs.append(get(tmp_ref, pl.ds(0, w, stride=2)) + get(tmp_ref, pl.ds(1, w, stride=2)))
                rows = pairs
            for row in rows:
                cells_ref[offset : offset + w, :] = row * (4.0**-level)
                offset += w
        cells16_ref[...] = cells_ref[...].astype(BF16)
        coarse_ref[...] = jnp.zeros_like(coarse_ref)
        qpad_ref[...] = jnp.zeros_like(qpad_ref)

    grads = a_ref[...]
    query = lax.dot_general(grads, cells16_ref[...], (((0,), (0,)), ((), ())), preferred_element_type=F32) * scale
    coarse_ref[...] += jnp.dot(grads, q_ref[...], preferred_element_type=F32)
    for half in range(q_ref.shape[0] // width):
        qpad_ref[8 : 8 + width, :] = query[half * width : (half + 1) * width]
        for k in range(n_ka):
            stage_ref[z ^ k, 0 : tile_q + 2, :] = qpad_ref[7 + tile_q * k : 9 + tile_q * (k + 1), :]
        for s in range(n_ka):
            q_outs[s][half] = stage_ref[s, 0 : tile_q + 2, :].astype(BF16)

    @pl.when(step == steps - 1)
    def _():
        offsets = [0]
        for level in range(LEVELS):
            offsets.append(offsets[-1] + (key_rows >> level) * (width >> level))
        finer = None
        for level in reversed(range(LEVELS)):
            w = width >> level
            here = []
            for r in range(key_rows >> level):
                start = offsets[level] + r * w
                value = coarse_ref[start : start + w, :] * (scale * 4.0**-level)
                if finer is not None:
                    value = value + finer[r // 2]
                here.append(value)
            if level:
                finer = []
                for value in here:
                    put(tmp_ref, pl.ds(0, w, stride=2), value)
                    put(tmp_ref, pl.ds(1, w, stride=2), value)
                    finer.append(get(tmp_ref, slice(0, 2 * w)))
        edge = jnp.zeros((key_rows, channels), F32)
        put(kpad_ref, slice(0, key_rows), edge)
        put(kpad_ref, slice((width + 1) * key_rows, (width + 2) * key_rows), edge)
        for r in range(key_rows):
            put(kpad_ref, pl.ds(key_rows + r, width, stride=key_rows), here[r])
        size = (tile_k + 2) * key_rows
        for s in range(n_quad):
            first = (quad ^ s) * 2 * tile_k * key_rows
            mine = pl.multiple_of(first + core * tile_k * key_rows, 8)
            other = pl.multiple_of(first + (1 - core) * tile_k * key_rows, 8)
            keep_ref[s] = get(kpad_ref, pl.ds(mine, size))
            send_ref[s] = get(kpad_ref, pl.ds(other, size)).astype(BF16)


def correlate(grads, queries, keys, width, key_rows, n_ka, n_quad):
    cells, count = grads.shape
    channels = queries.shape[1]
    rows = count // width
    tile_q = width // n_ka
    tile_k = width // (2 * n_quad)
    step_rows = 2
    size = (tile_k + 2) * key_rows
    whole2 = lambda i: (0, 0)
    whole3 = lambda i: (0, 0, 0)
    return pl.pallas_call(
        functools.partial(corr_kernel, width, key_rows, tile_q, tile_k, n_ka, n_quad),
        grid=(rows // step_rows,),
        in_specs=[
            pl.BlockSpec((cells, step_rows * width), lambda i: (0, i)),
            pl.BlockSpec((step_rows * width, channels), lambda i: (i, 0)),
            pl.BlockSpec((width * key_rows, channels), whole2),
        ],
        out_specs=[pl.BlockSpec((step_rows, tile_q + 2, channels), lambda i: (i, 0, 0))] * n_ka
        + [pl.BlockSpec((n_quad, size, channels), whole3)] * 2,
        out_shape=[jax.ShapeDtypeStruct((rows, tile_q + 2, channels), BF16)] * n_ka
        + [
            jax.ShapeDtypeStruct((n_quad, size, channels), BF16),
            jax.ShapeDtypeStruct((n_quad, size, channels), F32),
        ],
        scratch_shapes=[
            pltpu.VMEM((cells, channels), F32),
            pltpu.VMEM((cells, channels), BF16),
            pltpu.VMEM((cells, channels), F32),
            pltpu.VMEM((channels // 128, width * key_rows, 128), F32),
            pltpu.VMEM((channels // 128, width, 128), F32),
            pltpu.VMEM((channels // 128, (width + 2) * key_rows, 128), F32),
            pltpu.VMEM((width + 16, channels), F32),
            pltpu.VMEM((n_ka, tile_q + 8, channels), F32),
        ],
        compiler_params=pltpu.CompilerParams(vmem_limit_bytes=VMEM_BYTES),
        name="correlate",
    )(grads, queries, keys)


def fill(gq_ref, gtop_ref, gbot_ref, gk_ref, ktop_ref, kbot_ref, qext_ref, kext_ref):
    rows, wide, channels = gq_ref.shape
    tall = ktop_ref.shape[0]
    key_rows = gk_ref.shape[0] // tall
    qext_ref[0:1, 0:wide, :] = gtop_ref[...].astype(F32)
    qext_ref[1 : rows + 1, 0:wide, :] = gq_ref[...].astype(F32)
    qext_ref[rows + 1 : rows + 2, 0:wide, :] = gbot_ref[...].astype(F32)
    kext_ref[:, 8 : 8 + key_rows, :] = gk_ref[...].astype(F32).reshape(tall, key_rows, channels)
    kext_ref[:, 7:8, :] = ktop_ref[...].astype(F32)
    kext_ref[:, 8 + key_rows : 9 + key_rows, :] = kbot_ref[...].astype(F32)


def shifted(qext_ref, kext_ref, rows, tile_q, tile_k, key_rows, a, b):
    channels = qext_ref.shape[2]
    first = qext_ref[1 - a : 1 - a + rows, 1 - b : 1 - b + tile_q, :].reshape(rows * tile_q, channels)
    second = kext_ref[1 - b : 1 - b + tile_k, 8 - a : 8 - a + key_rows, :].reshape(tile_k * key_rows, channels)
    return jnp.concatenate([first.astype(BF16), second.astype(BF16)], axis=0)


def weight_kernel(gq, gtop, gbot, gk, ktop, kbot, qi_ref, ki_ref, send_ref, keep_ref, qext_ref, kext_ref, acc_ref):
    rows, wide, channels = gq.shape
    tall = ktop.shape[0]
    key_rows = gk.shape[0] // tall
    fill(gq, gtop, gbot, gk, ktop, kbot, qext_ref, kext_ref)
    cin = qi_ref.shape[1]
    image = jnp.concatenate([qi_ref[...].astype(F32).T, ki_ref[...].astype(F32).T], axis=1).astype(BF16)
    for tap in range(9):
        a, b = tap // 3 - 1, tap % 3 - 1
        grad = shifted(qext_ref, kext_ref, rows, wide - 2, tall - 2, key_rows, a, b)
        acc_ref[tap * cin : (tap + 1) * cin, :] = jnp.dot(image, grad, preferred_element_type=F32)
    half = send_ref.shape[0]
    core = lax.axis_index("pb") % 2
    keep_ref[...] = acc_ref[pl.ds(pl.multiple_of(core * half, 8), half), :]
    send_ref[...] = acc_ref[pl.ds(pl.multiple_of((1 - core) * half, 8), half), :].astype(BF16)


def image_kernel(gq, gtop, gbot, gk, ktop, kbot, w_ref, qo_ref, ko_ref, qext_ref, kext_ref):
    rows, wide, channels = gq.shape
    tall = ktop.shape[0]
    key_rows = gk.shape[0] // tall
    fill(gq, gtop, gbot, gk, ktop, kbot, qext_ref, kext_ref)
    total = None
    for tap in range(9):
        a, b = tap // 3 - 1, tap % 3 - 1
        grad = shifted(qext_ref, kext_ref, rows, wide - 2, tall - 2, key_rows, a, b)
        part = lax.dot_general(grad, w_ref[tap], (((1,), (1,)), ((), ())), preferred_element_type=F32)
        total = part if total is None else total + part
    count = qo_ref.shape[0]
    qo_ref[...] = total[:count].astype(BF16)
    ko_ref[...] = total[count:].astype(BF16)


def body(query_features, key_features, pyramid_grad, query_image, key_image, conv_weight):
    n_pb = lax.axis_size("pb")
    n_ka = lax.axis_size("ka")
    n_quad = n_pb // 2
    pb = lax.axis_index("pb")
    z = lax.axis_index("ka")
    core = pb % 2
    quad = pb // 2
    strip_rows, width, channels = query_features.shape
    key_rows = key_features.shape[1]
    cin = conv_weight.shape[2]
    tile_q = width // n_ka
    tile_k = width // n_pb
    sibling = flip(n_pb, 1)

    grads = jnp.transpose(pyramid_grad.reshape(pyramid_grad.shape[0], pyramid_grad.shape[2]))
    *q_parts, k_send, k_keep = correlate(
        grads,
        query_features.reshape(strip_rows * width, channels),
        key_features.reshape(width * key_rows, channels),
        width,
        key_rows,
        n_ka,
        n_quad,
    )
    k_recv = lax.ppermute(k_send, "pb", sibling)
    q_recv = [lax.ppermute(q_parts[s], "ka", flip(n_ka, s)) for s in range(1, n_ka)]
    k_pair = [k_keep[s] + k_recv[s].astype(F32) for s in range(n_quad)]
    k_more = [lax.ppermute(k_pair[s].astype(BF16), "pb", flip(n_pb, 2 * s)) for s in range(1, n_quad)]
    gq = sum([x.astype(F32) for x in q_recv], q_parts[0].astype(F32)).astype(BF16)
    gk = sum([x.astype(F32) for x in k_more], k_pair[0]).astype(BF16)

    first, last = gq[:1], gq[strip_rows - 1 :]
    lower = core == 0
    from_sibling = lax.ppermute(jnp.where(lower, last, first), "pb", sibling)
    links = [(i, i + 1) for i in range(1, n_pb - 1, 2)]
    from_remote = lax.ppermute(jnp.where(lower, first, last), "pb", links + [(d, s) for s, d in links])
    gtop = jnp.where(lower, from_remote, from_sibling)
    gbot = jnp.where(lower, from_sibling, from_remote)
    gk_rows = gk.reshape(tile_k + 2, key_rows, channels)
    ups = [(i, i + 1) for i in range(n_ka - 1)]
    ktop = lax.ppermute(gk_rows[:, key_rows - 1 :], "ka", ups)
    kbot = lax.ppermute(gk_rows[:, :1], "ka", [(d, s) for s, d in ups])

    around = (gq, gtop, gbot, gk, ktop, kbot)
    ext = [
        pltpu.VMEM((strip_rows + 2, tile_q + 16 - tile_q % 8, channels), F32),
        pltpu.VMEM((tile_k + 2, key_rows + 16, channels), F32),
    ]
    taps = 9
    half = taps * cin // 2
    w_send, w_keep = pl.pallas_call(
        weight_kernel,
        out_shape=[jax.ShapeDtypeStruct((half, channels), BF16), jax.ShapeDtypeStruct((half, channels), F32)],
        scratch_shapes=ext + [pltpu.VMEM((taps * cin, channels), F32)],
        compiler_params=pltpu.CompilerParams(vmem_limit_bytes=VMEM_BYTES),
        name="weights",
    )(*around, query_image.reshape(-1, cin), key_image.reshape(-1, cin))
    q_out, k_out = pl.pallas_call(
        image_kernel,
        out_shape=[jax.ShapeDtypeStruct((strip_rows * tile_q, cin), BF16), jax.ShapeDtypeStruct((tile_k * key_rows, cin), BF16)],
        scratch_shapes=ext,
        compiler_params=pltpu.CompilerParams(vmem_limit_bytes=VMEM_BYTES),
        name="images",
    )(*around, conv_weight.reshape(taps, cin, channels))

    pair = w_keep + lax.ppermute(w_send, "pb", sibling).astype(F32)
    pieces = pair.reshape(n_quad, half // n_quad, channels)
    got = [lax.ppermute(pick(pieces, quad ^ s).astype(BF16), "pb", flip(n_pb, 2 * s)) for s in range(1, n_quad)]
    part = sum([x.astype(F32) for x in got], pick(pieces, quad))
    pieces = part.reshape(n_ka, half // (n_quad * n_ka), channels)
    got = [lax.ppermute(pick(pieces, z ^ s).astype(BF16), "ka", flip(n_ka, s)) for s in range(1, n_ka)]
    part = sum([x.astype(F32) for x in got], pick(pieces, z)).astype(BF16)
    part = jnp.concatenate(
        ordered([part] + [lax.ppermute(part, "ka", flip(n_ka, s)) for s in range(1, n_ka)], z), axis=0
    )
    part = jnp.concatenate(
        ordered([part] + [lax.ppermute(part, "pb", flip(n_pb, 2 * s)) for s in range(1, n_quad)], quad), axis=0
    )
    whole = jnp.concatenate(ordered([part, lax.ppermute(part, "pb", sibling)], core), axis=0)
    weight_grad = whole.astype(F32).reshape(conv_weight.shape)
    return (
        q_out.reshape(query_image.shape),
        k_out.reshape(key_image.shape),
        weight_grad,
    )


def solution(mesh):
    placed = (
        P("pb", None, None),
        P(None, "ka", None),
        P("pb", "ka", None),
        P("pb", "ka", None),
        P("pb", "ka", None),
        P(),
    )
    return jax.shard_map(
        body,
        mesh=mesh,
        in_specs=placed,
        out_specs=(P("pb", "ka", None), P("pb", "ka", None), P()),
        check_vma=False,
    )
```

```python
import functools

import jax
import jax.numpy as jnp
from jax import lax
from jax.experimental import pallas as pl
from jax.experimental.pallas import tpu as pltpu
from jax.sharding import PartitionSpec as P

LEVELS = 4
F32 = jnp.float32
BF16 = jnp.bfloat16
SMALL_BYTES = 16 * 2**20


def flip(count, mask):
    return [(i, i ^ mask) for i in range(count)]


def ordered(parts, index):
    count = len(parts)
    bit = 1
    while bit < count:
        swap = (index & bit) != 0
        parts = [jnp.where(swap, parts[a ^ bit], parts[a]) for a in range(count)]
        bit *= 2
    return parts


def put(ref, rows, value):
    for lane in range(ref.shape[0]):
        ref[lane, rows, :] = value[:, lane * 128 : (lane + 1) * 128]


def get(ref, rows):
    return jnp.concatenate([ref[lane, rows, :] for lane in range(ref.shape[0])], axis=1)


def up16(count):
    return -(-count // 16) * 16


def joins(mask):
    return (mask & (mask + 1)) == 0


def place():
    pb = lax.axis_index("pb")
    return pb // 2, pb % 2, lax.axis_index("ka")


def carried(parts, index, step):
    total = None
    for mask, row in parts:
        row = jnp.where((index ^ mask) == index + step, row, 0.0)
        total = row if total is None else total + row
    return total


def corr_kernel(dims, a_hbm, q_hbm, key_hbm, qi_hbm, ki_hbm, *rest):
    width, key_rows, tile_q, tile_k, n_ka, n_quad, chunk = dims
    q_outs = rest[:n_ka]
    send_ref, keep_ref = rest[n_ka : n_ka + 2]
    a_ref, q_ref, key_ref, cells_ref, coarse_ref, keyf_ref, tmp_ref, kpad_ref, qpad_ref, stage_ref, qi_ref, ki_ref, sems = rest[n_ka + 2 :]
    count, channels = q_ref.shape
    rows = count // width
    scale = channels ** (-0.5)
    quad, core, z = place()

    copies = [pltpu.make_async_copy(key_hbm, key_ref, sems.at[0])]
    for i in range(count // chunk):
        lanes = pl.ds(i * chunk, chunk)
        copies.append(pltpu.make_async_copy(a_hbm.at[:, lanes], a_ref.at[:, lanes], sems.at[i + 2]))
    copies.append(pltpu.make_async_copy(q_hbm, q_ref, sems.at[1]))
    copies.append(pltpu.make_async_copy(qi_hbm, qi_ref, sems.at[count // chunk + 2]))
    copies.append(pltpu.make_async_copy(ki_hbm, ki_ref, sems.at[count // chunk + 3]))
    for copy in copies:
        copy.start()

    qpad_ref[...] = jnp.zeros_like(qpad_ref)
    edge = jnp.zeros((key_rows, channels), F32)
    put(kpad_ref, slice(0, key_rows), edge)
    put(kpad_ref, slice((width + 1) * key_rows, (width + 2) * key_rows), edge)

    copies[0].wait()
    put(keyf_ref, slice(None), key_ref[...].astype(F32))
    lines = [get(keyf_ref, pl.ds(r, width, stride=key_rows)) for r in range(key_rows)]
    offset = 0
    for level in range(LEVELS):
        w = width >> level
        if level:
            pairs = []
            for i in range(len(lines) // 2):
                put(tmp_ref, slice(0, 2 * w), lines[2 * i] + lines[2 * i + 1])
                pairs.append(get(tmp_ref, pl.ds(0, w, stride=2)) + get(tmp_ref, pl.ds(1, w, stride=2)))
            lines = pairs
        for line in lines:
            cells_ref[offset : offset + w, :] = line * (4.0**-level)
            offset += w
    cells = cells_ref[...].astype(BF16)
    for copy in copies[1:]:
        copy.wait()

    last_row = ki_ref[...].astype(F32)
    first_row, last_row = last_row[:, 0], last_row[:, key_rows - 1]
    for s in range(1, n_ka):
        if joins(s):
            q_outs[s][rows, 0:tile_k] = jnp.where((z ^ s) == z + 1, last_row, first_row).astype(BF16)
    base = n_quad * (tile_k + 2) * key_rows
    send_ref[base : base + tile_q, :] = qi_ref[0]
    send_ref[base + up16(tile_q) : base + up16(tile_q) + tile_q, :] = qi_ref[rows - 1]
    query = lax.dot_general(cells, a_ref[...], (((0,), (0,)), ((), ())), preferred_element_type=F32).T * scale
    coarse_ref[...] = jnp.dot(a_ref[...], q_ref[...], preferred_element_type=F32)
    for row in range(rows):
        qpad_ref[8 : 8 + width, :] = query[row * width : (row + 1) * width]
        for k in range(n_ka):
            stage_ref[z ^ k, 0 : tile_q + 2, :] = qpad_ref[7 + tile_q * k : 9 + tile_q * (k + 1), :]
        for s in range(n_ka):
            q_outs[s][row] = stage_ref[s, 0 : tile_q + 2, :].astype(BF16)

    offsets = [0]
    for level in range(LEVELS):
        offsets.append(offsets[-1] + (key_rows >> level) * (width >> level))
    finer = None
    for level in reversed(range(LEVELS)):
        w = width >> level
        here = []
        for r in range(key_rows >> level):
            start = offsets[level] + r * w
            value = coarse_ref[start : start + w, :] * (scale * 4.0**-level)
            if finer is not None:
                value = value + finer[r // 2]
            here.append(value)
        if level:
            finer = []
            for value in here:
                put(tmp_ref, pl.ds(0, w, stride=2), value)
                put(tmp_ref, pl.ds(1, w, stride=2), value)
                finer.append(get(tmp_ref, slice(0, 2 * w)))
    for r in range(key_rows):
        put(kpad_ref, pl.ds(key_rows + r, width, stride=key_rows), here[r])
    size = (tile_k + 2) * key_rows
    for s in range(n_quad):
        first = (quad ^ s) * 2 * tile_k * key_rows
        mine = pl.multiple_of(first + core * tile_k * key_rows, 8)
        other = pl.multiple_of(first + (1 - core) * tile_k * key_rows, 8)
        keep_ref[s] = get(kpad_ref, pl.ds(mine, size))
        send_ref[s * size : (s + 1) * size, :] = get(kpad_ref, pl.ds(other, size)).astype(BF16)


def correlate(grads, queries, keys, query_image, key_image, width, key_rows, n_ka, n_quad):
    cells, count = grads.shape
    channels = queries.shape[1]
    rows = count // width
    tile_q = width // n_ka
    tile_k = width // (2 * n_quad)
    size = (tile_k + 2) * key_rows
    chunk = 256
    hbm = pl.BlockSpec(memory_space=pltpu.HBM)
    vmem = pl.BlockSpec(memory_space=pltpu.VMEM)
    dims = (width, key_rows, tile_q, tile_k, n_ka, n_quad, chunk)
    lanes = channels // 128
    return pl.pallas_call(
        functools.partial(corr_kernel, dims),
        in_specs=[hbm] * 5,
        out_specs=[vmem] * (n_ka + 2),
        out_shape=[jax.ShapeDtypeStruct((rows + (s > 0 and joins(s)), tile_q + 2, channels), BF16) for s in range(n_ka)]
        + [
            jax.ShapeDtypeStruct((n_quad * size + 2 * up16(tile_q), channels), BF16),
            jax.ShapeDtypeStruct((n_quad, size, channels), F32),
        ],
        scratch_shapes=[
            pltpu.VMEM((cells, count), BF16),
            pltpu.VMEM((count, channels), BF16),
            pltpu.VMEM((width * key_rows, channels), BF16),
            pltpu.VMEM((cells, channels), F32),
            pltpu.VMEM((cells, channels), F32),
            pltpu.VMEM((lanes, width * key_rows, 128), F32),
            pltpu.VMEM((lanes, width, 128), F32),
            pltpu.VMEM((lanes, (width + 2) * key_rows, 128), F32),
            pltpu.VMEM((width + 16, channels), F32),
            pltpu.VMEM((n_ka, tile_q + 8, channels), F32),
            pltpu.VMEM(query_image.shape, BF16),
            pltpu.VMEM(key_image.shape, BF16),
            pltpu.SemaphoreType.DMA((count // chunk + 4,)),
        ],
        compiler_params=pltpu.CompilerParams(vmem_limit_bytes=cells * (count * 4 + channels * 24)),
        name="correlate",
    )(*[pltpu.with_memory_space_constraint(x, pltpu.HBM) for x in (grads, queries, keys, query_image, key_image)])


def pair_kernel(size, tile, keep_ref, recv_ref, own_ref, near_ref, *sends):
    quad, core, _ = place()
    n_quad = len(sends) + 1
    base = n_quad * size
    first = recv_ref[base : base + tile, :].astype(F32)
    last = recv_ref[base + up16(tile) : base + up16(tile) + tile, :].astype(F32)
    near_ref[...] = jnp.where(core == 0, first, last).astype(BF16)
    onward = jnp.where(core == 0, last, first).astype(BF16)
    own_ref[...] = keep_ref[0] + recv_ref[0:size, :].astype(F32)
    for s, send in enumerate(sends, 1):
        send[0:size, :] = (keep_ref[s] + recv_ref[s * size : (s + 1) * size, :].astype(F32)).astype(BF16)
        if joins(s):
            send[size : size + tile, :] = onward


def both_sides(refs, near_ref, size, quad, core):
    tile = near_ref.shape[0]
    parts = [(s, ref[size : size + tile, :].astype(F32)) for s, ref in enumerate(refs, 1) if joins(s)]
    near = near_ref[...].astype(F32)
    far = carried(parts, quad, 2 * core - 1)
    return jnp.where(core == 0, far, near), jnp.where(core == 0, near, far)


def weight_kernel(n_ka, n_quad, *refs):
    q_refs = refs[:n_ka]
    k_refs = refs[n_ka : n_ka + n_quad]
    near_ref, qi_ref, ki_ref = refs[n_ka + n_quad : n_ka + n_quad + 3]
    send_ref, keep_ref, gq_ref, gk_ref, acc_ref, sum_ref, ext_ref = refs[n_ka + n_quad + 3 :]
    rows, wide, channels = gq_ref.shape
    size = gk_ref.shape[0]
    tile_k, key_rows, cin = ki_ref.shape
    tile_q = wide - 2
    quad, core, z = place()
    top, bottom = both_sides(k_refs[1:], near_ref, size, quad, core)
    lines = [(s, ref[rows, 0:tile_k].astype(F32)) for s, ref in enumerate(q_refs) if s and joins(s)]
    ext_ref[:, 8 : 8 + key_rows, :] = ki_ref[...].astype(F32)
    ext_ref[:, 7, :] = carried(lines, z, -1)
    ext_ref[:, 8 + key_rows, :] = carried(lines, z, 1)
    query = jnp.concatenate([top[None], qi_ref[...].astype(F32), bottom[None]], axis=0)
    image = []
    for a in (-1, 0, 1):
        first = query[1 + a : 1 + a + rows].reshape(rows * tile_q, cin)
        second = ext_ref[:, 8 + a : 8 + a + key_rows, :].reshape(tile_k * key_rows, cin)
        image.append(jnp.concatenate([first, second], axis=0).T.astype(BF16))
    image = jnp.concatenate(image, axis=0)
    query = q_refs[0][...].astype(F32)
    for ref in q_refs[1:]:
        query = query + ref[0:rows].astype(F32)
    gq = query.astype(BF16)
    gq_ref[...] = gq
    sum_ref[:, 0:wide, :] = gq.astype(F32)
    key = k_refs[0][...]
    for ref in k_refs[1:]:
        key = key + ref[0:size, :].astype(F32)
    gk = key.astype(BF16)
    gk_ref[...] = gk
    count = tile_k * key_rows
    for b in (-1, 0, 1):
        first = sum_ref[:, 1 - b : 1 - b + tile_q, :].reshape(rows * tile_q, channels).astype(BF16)
        grad = jnp.concatenate([first, gk[(1 - b) * key_rows : (1 - b) * key_rows + count]], axis=0)
        part = jnp.dot(image, grad, preferred_element_type=F32)
        for a in range(3):
            tap = a * 3 + b + 1
            acc_ref[tap * cin : (tap + 1) * cin, :] = part[a * cin : (a + 1) * cin]
    half = keep_ref.shape[0]
    keep_ref[...] = acc_ref[pl.ds(pl.multiple_of(core * half, 16), half), :]
    send_ref[0:half, :] = acc_ref[pl.ds(pl.multiple_of((1 - core) * half, 16), half), :].astype(BF16)
    send_ref[half : half + wide, :] = gq[0]
    send_ref[half + up16(wide) : half + up16(wide) + wide, :] = gq[rows - 1]


def piece_kernel(keep_ref, recv_ref, own_ref, near_ref, *rest):
    *sends, sum_ref = rest
    quad, core, _ = place()
    half = keep_ref.shape[0]
    size = own_ref.shape[0]
    tile = near_ref.shape[0]
    first = recv_ref[half : half + tile, :].astype(F32)
    last = recv_ref[half + up16(tile) : half + up16(tile) + tile, :].astype(F32)
    near_ref[...] = jnp.where(core == 0, first, last).astype(BF16)
    onward = jnp.where(core == 0, last, first).astype(BF16)
    sum_ref[...] = keep_ref[...] + recv_ref[0:half, :].astype(F32)
    own_ref[...] = sum_ref[pl.ds(pl.multiple_of(quad * size, 16), size), :]
    for s, send in enumerate(sends, 1):
        send[0:size, :] = sum_ref[pl.ds(pl.multiple_of((quad ^ s) * size, 16), size), :].astype(BF16)
        if joins(s):
            send[size : size + tile, :] = onward


def layer_kernel(n_quad, n_ka, *refs):
    own_ref, *got = refs[:n_quad]
    near_ref, gk_ref, out_ref, top_ref, bottom_ref = refs[n_quad : n_quad + 5]
    sends = refs[n_quad + 5 : n_quad + 4 + n_ka]
    stage_ref, ext_ref = refs[n_quad + 4 + n_ka :]
    quad, core, z = place()
    size = own_ref.shape[0]
    piece = size // n_ka
    top, bottom = both_sides(got, near_ref, size, quad, core)
    top_ref[...] = top.astype(BF16)
    bottom_ref[...] = bottom.astype(BF16)
    total = own_ref[...]
    for ref in got:
        total = total + ref[0:size, :].astype(F32)
    for k in range(n_ka):
        stage_ref[z ^ k, 0:piece, :] = total[k * piece : (k + 1) * piece]
    out_ref[...] = stage_ref[0, 0:piece, :]
    tall, key_rows, _ = ext_ref.shape
    ext_ref[...] = gk_ref[...].astype(F32).reshape(ext_ref.shape)
    first, last = ext_ref[:, 0, :], ext_ref[:, key_rows - 1, :]
    for s, send in enumerate(sends, 1):
        send[0:piece, :] = stage_ref[s, 0:piece, :].astype(BF16)
        if joins(s):
            send[piece : piece + tall, :] = jnp.where((z ^ s) == z + 1, last, first).astype(BF16)


def image_kernel(piece, gq_ref, top_ref, bottom_ref, gk_ref, w_ref, *rest):
    *got, qo_ref, ko_ref, qext_ref, kext_ref = rest
    rows, wide, channels = gq_ref.shape
    tall = kext_ref.shape[0]
    key_rows = gk_ref.shape[0] // tall
    tile_q = wide - 2
    tile_k = tall - 2
    _, _, z = place()
    lines = [(s, ref[piece : piece + tall, :].astype(F32)) for s, ref in enumerate(got, 1) if joins(s)]
    qext_ref[0, 0:wide, :] = top_ref[...].astype(F32)
    qext_ref[1 : rows + 1, 0:wide, :] = gq_ref[...].astype(F32)
    qext_ref[rows + 1, 0:wide, :] = bottom_ref[...].astype(F32)
    kext_ref[:, 8 : 8 + key_rows, :] = gk_ref[...].astype(F32).reshape(tall, key_rows, channels)
    kext_ref[:, 7, :] = carried(lines, z, -1)
    kext_ref[:, 8 + key_rows, :] = carried(lines, z, 1)
    total = None
    for tap in range(9):
        a, b = tap // 3 - 1, tap % 3 - 1
        first = qext_ref[1 - a : 1 - a + rows, 1 - b : 1 - b + tile_q, :].reshape(rows * tile_q, channels)
        second = kext_ref[1 - b : 1 - b + tile_k, 8 - a : 8 - a + key_rows, :].reshape(tile_k * key_rows, channels)
        grad = jnp.concatenate([first.astype(BF16), second.astype(BF16)], axis=0)
        part = lax.dot_general(grad, w_ref[tap], (((1,), (1,)), ((), ())), preferred_element_type=F32)
        total = part if total is None else total + part
    count = qo_ref.shape[0]
    qo_ref[...] = total[:count].astype(BF16)
    ko_ref[...] = total[count:].astype(BF16)


def call(kernel, name, outs, args, scratch=()):
    return pl.pallas_call(
        kernel,
        in_specs=[pl.BlockSpec(memory_space=pltpu.VMEM)] * len(args),
        out_shape=[jax.ShapeDtypeStruct(shape, dtype) for shape, dtype in outs],
        scratch_shapes=[pltpu.VMEM(shape, F32) for shape in scratch],
        compiler_params=pltpu.CompilerParams(vmem_limit_bytes=SMALL_BYTES),
        name=name,
    )(*args)


def body(query_features, key_features, pyramid_grad, query_image, key_image, conv_weight):
    n_pb = lax.axis_size("pb")
    n_ka = lax.axis_size("ka")
    n_quad = n_pb // 2
    quad, core, z = place()
    strip_rows, width, channels = query_features.shape
    key_rows = key_features.shape[1]
    cin = conv_weight.shape[2]
    tile_q = width // n_ka
    tile_k = width // n_pb
    wide = tile_q + 2
    tall = tile_k + 2
    size = tall * key_rows
    taps = 9
    half = taps * cin // 2
    quarter = half // n_quad
    piece = quarter // n_ka

    def to_core(x):
        return lax.ppermute(x, "pb", flip(n_pb, 1))

    def to_quad(parts):
        return [lax.ppermute(x, "pb", flip(n_pb, 2 * s)) for s, x in enumerate(parts, 1)]

    def to_layers(parts):
        return [lax.ppermute(x, "ka", flip(n_ka, s)) for s, x in enumerate(parts, 1)]

    def extra(count, mask, more):
        return count + (more if joins(mask) else 0)

    grads = jnp.transpose(pyramid_grad.reshape(pyramid_grad.shape[0], pyramid_grad.shape[2]))
    *q_parts, k_send, k_keep = correlate(
        grads,
        query_features.reshape(strip_rows * width, channels),
        key_features.reshape(width * key_rows, channels),
        query_image,
        key_image,
        width,
        key_rows,
        n_ka,
        n_quad,
    )
    k_recv = to_core(k_send)
    q_recv = to_layers(q_parts[1:])
    outs = [((size, channels), F32), ((tile_q, cin), BF16)]
    outs += [((extra(size, s, tile_q), channels), BF16) for s in range(1, n_quad)]
    k_own, near, *k_pair = call(functools.partial(pair_kernel, size, tile_q), "pairs", outs, (k_keep, k_recv))
    k_more = to_quad(k_pair)
    outs = [
        ((half + 2 * up16(wide), channels), BF16),
        ((half, channels), F32),
        ((strip_rows, wide, channels), BF16),
        ((size, channels), BF16),
    ]
    w_send, w_keep, gq, gk = call(
        functools.partial(weight_kernel, n_ka, n_quad),
        "weights",
        outs,
        (q_parts[0], *q_recv, k_own, *k_more, near, query_image, key_image),
        [(taps * cin, channels), (strip_rows, up16(wide), channels), (tile_k, key_rows + 16, cin)],
    )

    w_recv = to_core(w_send)
    outs = [((quarter, channels), F32), ((wide, channels), BF16)]
    outs += [((extra(quarter, s, wide), channels), BF16) for s in range(1, n_quad)]
    own, near, *sends = call(piece_kernel, "pieces", outs, (w_keep, w_recv), [(half, channels)])
    got = to_quad(sends)
    outs = [((piece, channels), F32)] + [((wide, channels), BF16)] * 2
    outs += [((extra(piece, s, tall), channels), BF16) for s in range(1, n_ka)]
    own, top, bottom, *sends = call(
        functools.partial(layer_kernel, n_quad, n_ka),
        "layers",
        outs,
        (own, *got, near, gk),
        [(n_ka, up16(piece), channels), (tall, key_rows, channels)],
    )
    got = to_layers(sends)
    part = sum([x[:piece].astype(F32) for x in got], own).astype(BF16)
    q_out, k_out = call(
        functools.partial(image_kernel, piece),
        "images",
        [((strip_rows * tile_q, cin), BF16), ((tile_k * key_rows, cin), BF16)],
        (gq, top, bottom, gk, conv_weight.reshape(taps, cin, channels), *got),
        [(strip_rows + 2, up16(wide), channels), (tall, key_rows + 16, channels)],
    )
    part = jnp.concatenate(ordered([part] + to_layers([part] * (n_ka - 1)), z), axis=0)
    part = jnp.concatenate(ordered([part] + to_quad([part] * (n_quad - 1)), quad), axis=0)
    whole = jnp.concatenate(ordered([part, to_core(part)], core), axis=0)
    return (
        q_out.reshape(query_image.shape),
        k_out.reshape(key_image.shape),
        whole.astype(F32).reshape(conv_weight.shape),
    )


def solution(mesh):
    placed = (
        P("pb", None, None),
        P(None, "ka", None),
        P("pb", "ka", None),
        P("pb", "ka", None),
        P("pb", "ka", None),
        P(),
    )
    return jax.shard_map(
        body,
        mesh=mesh,
        in_specs=placed,
        out_specs=(P("pb", "ka", None), P("pb", "ka", None), P()),
        check_vma=False,
    )
```

```python
import functools

import jax
import jax.numpy as jnp
from jax import lax
from jax.experimental import pallas as pl
from jax.experimental.pallas import tpu as pltpu
from jax.sharding import PartitionSpec as P

LEVELS = 4
F32 = jnp.float32
BF16 = jnp.bfloat16
SMALL_BYTES = 16 * 2**20


def flip(count, mask):
    return [(i, i ^ mask) for i in range(count)]


def put(ref, rows, value):
    for lane in range(ref.shape[0]):
        ref[lane, rows, :] = value[:, lane * 128 : (lane + 1) * 128]


def get(ref, rows):
    return jnp.concatenate([ref[lane, rows, :] for lane in range(ref.shape[0])], axis=1)


def up16(count):
    return -(-count // 16) * 16


def joins(mask):
    return (mask & (mask + 1)) == 0


def place():
    pb = lax.axis_index("pb")
    return pb // 2, pb % 2, lax.axis_index("ka")


def carried(parts, index, step):
    total = None
    for mask, row in parts:
        row = jnp.where((index ^ mask) == index + step, row, 0.0)
        total = row if total is None else total + row
    return total


def corr_kernel(dims, a_hbm, q_hbm, key_hbm, qi_hbm, ki_hbm, *rest):
    width, key_rows, tile_q, tile_k, n_ka, n_quad, chunk = dims
    q_outs = rest[:n_ka]
    send_ref, keep_ref = rest[n_ka : n_ka + 2]
    a_ref, q_ref, key_ref, cells_ref, coarse_ref, keyf_ref, tmp_ref, kpad_ref, qpad_ref, stage_ref, qi_ref, ki_ref, sems = rest[n_ka + 2 :]
    count, channels = q_ref.shape
    rows = count // width
    scale = channels ** (-0.5)
    quad, core, z = place()

    copies = [pltpu.make_async_copy(key_hbm, key_ref, sems.at[0])]
    for i in range(count // chunk):
        lanes = pl.ds(i * chunk, chunk)
        copies.append(pltpu.make_async_copy(a_hbm.at[:, lanes], a_ref.at[:, lanes], sems.at[i + 2]))
    copies.append(pltpu.make_async_copy(q_hbm, q_ref, sems.at[1]))
    copies.append(pltpu.make_async_copy(qi_hbm, qi_ref, sems.at[count // chunk + 2]))
    copies.append(pltpu.make_async_copy(ki_hbm, ki_ref, sems.at[count // chunk + 3]))
    for copy in copies:
        copy.start()

    qpad_ref[...] = jnp.zeros_like(qpad_ref)
    edge = jnp.zeros((key_rows, channels), F32)
    put(kpad_ref, slice(0, key_rows), edge)
    put(kpad_ref, slice((width + 1) * key_rows, (width + 2) * key_rows), edge)

    copies[0].wait()
    put(keyf_ref, slice(None), key_ref[...].astype(F32))
    lines = [get(keyf_ref, pl.ds(r, width, stride=key_rows)) for r in range(key_rows)]
    offset = 0
    for level in range(LEVELS):
        w = width >> level
        if level:
            pairs = []
            for i in range(len(lines) // 2):
                put(tmp_ref, slice(0, 2 * w), lines[2 * i] + lines[2 * i + 1])
                pairs.append(get(tmp_ref, pl.ds(0, w, stride=2)) + get(tmp_ref, pl.ds(1, w, stride=2)))
            lines = pairs
        for line in lines:
            cells_ref[offset : offset + w, :] = line * (4.0**-level)
            offset += w
    cells = cells_ref[...].astype(BF16)
    for copy in copies[1:]:
        copy.wait()
    query = lax.dot_general(cells, a_ref[...], (((0,), (0,)), ((), ())), preferred_element_type=F32).T * scale

    last_row = ki_ref[...].astype(F32)
    first_row, last_row = last_row[:, 0], last_row[:, key_rows - 1]
    wide = tile_q + 2
    for s in range(1, n_ka):
        if joins(s):
            stage_ref[s, rows * wide : rows * wide + tile_k, :] = jnp.where((z ^ s) == z + 1, last_row, first_row)
    base = n_quad * (tile_k + 2) * key_rows
    send_ref[base : base + tile_q, :] = qi_ref[0]
    send_ref[base + up16(tile_q) : base + up16(tile_q) + tile_q, :] = qi_ref[rows - 1]
    coarse_ref[...] = jnp.dot(a_ref[...], q_ref[...], preferred_element_type=F32)
    for row in range(rows):
        qpad_ref[8 : 8 + width, :] = query[row * width : (row + 1) * width]
        for k in range(n_ka):
            stage_ref[z ^ k, row * wide : (row + 1) * wide, :] = qpad_ref[7 + tile_q * k : 9 + tile_q * (k + 1), :]
    for s in range(n_ka):
        q_outs[s][...] = stage_ref[s, 0 : q_outs[s].shape[0], :].astype(BF16)

    offsets = [0]
    for level in range(LEVELS):
        offsets.append(offsets[-1] + (key_rows >> level) * (width >> level))
    finer = None
    for level in reversed(range(LEVELS)):
        w = width >> level
        here = []
        for r in range(key_rows >> level):
            start = offsets[level] + r * w
            value = coarse_ref[start : start + w, :] * (scale * 4.0**-level)
            if finer is not None:
                value = value + finer[r // 2]
            here.append(value)
        if level:
            finer = []
            for value in here:
                put(tmp_ref, pl.ds(0, w, stride=2), value)
                put(tmp_ref, pl.ds(1, w, stride=2), value)
                finer.append(get(tmp_ref, slice(0, 2 * w)))
    for r in range(key_rows):
        put(kpad_ref, pl.ds(key_rows + r, width, stride=key_rows), here[r])
    size = (tile_k + 2) * key_rows
    for s in range(n_quad):
        first = (quad ^ s) * 2 * tile_k * key_rows
        mine = pl.multiple_of(first + core * tile_k * key_rows, 8)
        other = pl.multiple_of(first + (1 - core) * tile_k * key_rows, 8)
        keep_ref[s] = get(kpad_ref, pl.ds(mine, size))
        send_ref[s * size : (s + 1) * size, :] = get(kpad_ref, pl.ds(other, size)).astype(BF16)


def correlate(grads, queries, keys, query_image, key_image, width, key_rows, n_ka, n_quad):
    cells, count = grads.shape
    channels = queries.shape[1]
    rows = count // width
    tile_q = width // n_ka
    tile_k = width // (2 * n_quad)
    size = (tile_k + 2) * key_rows
    counts = [rows * (tile_q + 2) + (tile_k if s and joins(s) else 0) for s in range(n_ka)]
    chunk = 256
    hbm = pl.BlockSpec(memory_space=pltpu.HBM)
    vmem = pl.BlockSpec(memory_space=pltpu.VMEM)
    dims = (width, key_rows, tile_q, tile_k, n_ka, n_quad, chunk)
    lanes = channels // 128
    return pl.pallas_call(
        functools.partial(corr_kernel, dims),
        in_specs=[hbm] * 5,
        out_specs=[vmem] * (n_ka + 2),
        out_shape=[
            jax.ShapeDtypeStruct((count, channels), BF16) for count in counts
        ]
        + [
            jax.ShapeDtypeStruct((n_quad * size + 2 * up16(tile_q), channels), BF16),
            jax.ShapeDtypeStruct((n_quad, size, channels), F32),
        ],
        scratch_shapes=[
            pltpu.VMEM((cells, count), BF16),
            pltpu.VMEM((count, channels), BF16),
            pltpu.VMEM((width * key_rows, channels), BF16),
            pltpu.VMEM((cells, channels), F32),
            pltpu.VMEM((cells, channels), F32),
            pltpu.VMEM((lanes, width * key_rows, 128), F32),
            pltpu.VMEM((lanes, width, 128), F32),
            pltpu.VMEM((lanes, (width + 2) * key_rows, 128), F32),
            pltpu.VMEM((width + 16, channels), F32),
            pltpu.VMEM((n_ka, up16(max(counts)), channels), F32),
            pltpu.VMEM(query_image.shape, BF16),
            pltpu.VMEM(key_image.shape, BF16),
            pltpu.SemaphoreType.DMA((count // chunk + 4,)),
        ],
        compiler_params=pltpu.CompilerParams(vmem_limit_bytes=cells * (count * 4 + channels * 24)),
        name="correlate",
    )(*[pltpu.with_memory_space_constraint(x, pltpu.HBM) for x in (grads, queries, keys, query_image, key_image)])


def pair_kernel(size, tile, keep_ref, recv_ref, own_ref, near_ref, *sends):
    quad, core, _ = place()
    n_quad = len(sends) + 1
    base = n_quad * size
    first = recv_ref[base : base + tile, :].astype(F32)
    last = recv_ref[base + up16(tile) : base + up16(tile) + tile, :].astype(F32)
    near_ref[...] = jnp.where(core == 0, first, last).astype(BF16)
    onward = jnp.where(core == 0, last, first).astype(BF16)
    own_ref[...] = keep_ref[0] + recv_ref[0:size, :].astype(F32)
    for s, send in enumerate(sends, 1):
        send[0:size, :] = (keep_ref[s] + recv_ref[s * size : (s + 1) * size, :].astype(F32)).astype(BF16)
        if joins(s):
            send[size : size + tile, :] = onward


def both_sides(refs, near_ref, size, quad, core):
    tile = near_ref.shape[0]
    parts = [(s, ref[size : size + tile, :].astype(F32)) for s, ref in enumerate(refs, 1) if joins(s)]
    near = near_ref[...].astype(F32)
    far = carried(parts, quad, 2 * core - 1)
    return jnp.where(core == 0, far, near), jnp.where(core == 0, near, far)


def weight_kernel(n_ka, n_quad, *refs):
    q_refs = refs[:n_ka]
    k_refs = refs[n_ka : n_ka + n_quad]
    near_ref, qi_ref, ki_ref = refs[n_ka + n_quad : n_ka + n_quad + 3]
    send_ref, keep_ref, gq_ref, gk_ref, acc_ref, sum_ref, ext_ref = refs[n_ka + n_quad + 3 :]
    size, channels = gk_ref.shape
    tile_k, key_rows, cin = ki_ref.shape
    rows, tile_q, _ = qi_ref.shape
    wide = tile_q + 2
    quad, core, z = place()
    top, bottom = both_sides(k_refs[1:], near_ref, size, quad, core)
    lines = [(s, ref[rows * wide : rows * wide + tile_k, :].astype(F32)) for s, ref in enumerate(q_refs) if s and joins(s)]
    ext_ref[:, 8 : 8 + key_rows, :] = ki_ref[...].astype(F32)
    ext_ref[:, 7, :] = carried(lines, z, -1)
    ext_ref[:, 8 + key_rows, :] = carried(lines, z, 1)
    query = jnp.concatenate([top[None], qi_ref[...].astype(F32), bottom[None]], axis=0)
    image = []
    for a in (-1, 0, 1):
        first = query[1 + a : 1 + a + rows].reshape(rows * tile_q, cin)
        second = ext_ref[:, 8 + a : 8 + a + key_rows, :].reshape(tile_k * key_rows, cin)
        image.append(jnp.concatenate([first, second], axis=0).T.astype(BF16))
    image = jnp.concatenate(image, axis=0)
    query = q_refs[0][...].astype(F32)
    for ref in q_refs[1:]:
        query = query + ref[0 : rows * wide, :].astype(F32)
    gq = query.astype(BF16)
    gq_ref[...] = gq
    sum_ref[...] = gq.astype(F32)
    key = k_refs[0][...]
    for ref in k_refs[1:]:
        key = key + ref[0:size, :].astype(F32)
    gk = key.astype(BF16)
    gk_ref[...] = gk
    count = tile_k * key_rows
    for b in (-1, 0, 1):
        starts = [row * wide + 1 - b for row in range(rows)]
        first = jnp.concatenate([sum_ref[start : start + tile_q, :] for start in starts], axis=0).astype(BF16)
        grad = jnp.concatenate([first, gk[(1 - b) * key_rows : (1 - b) * key_rows + count]], axis=0)
        part = jnp.dot(image, grad, preferred_element_type=F32)
        for a in range(3):
            tap = a * 3 + b + 1
            acc_ref[tap * cin : (tap + 1) * cin, :] = part[a * cin : (a + 1) * cin]
    half = keep_ref.shape[0]
    keep_ref[...] = acc_ref[pl.ds(pl.multiple_of(core * half, 16), half), :]
    send_ref[0:half, :] = acc_ref[pl.ds(pl.multiple_of((1 - core) * half, 16), half), :].astype(BF16)
    first, last = sum_ref[0:wide, :], sum_ref[(rows - 1) * wide : rows * wide, :]
    send_ref[half : half + wide, :] = jnp.where(core == 0, last, first).astype(BF16)


def piece_kernel(keep_ref, recv_ref, own_ref, near_ref, *rest):
    *sends, sum_ref = rest
    quad, core, _ = place()
    half = keep_ref.shape[0]
    size = own_ref.shape[0]
    tile = near_ref.shape[0]
    near_ref[...] = recv_ref[half : half + tile, :]
    sum_ref[...] = keep_ref[...] + recv_ref[0:half, :].astype(F32)
    own_ref[...] = sum_ref[pl.ds(pl.multiple_of(quad * size, 16), size), :]
    for s, send in enumerate(sends, 1):
        send[...] = sum_ref[pl.ds(pl.multiple_of((quad ^ s) * size, 16), size), :].astype(BF16)


def layer_kernel(n_quad, rows, *refs):
    own_ref, *got = refs[:n_quad]
    gq_ref, out_ref, far_ref, *sends, stage_ref = refs[n_quad:]
    _, core, z = place()
    n_ka = len(sends) + 1
    size = own_ref.shape[0]
    piece = size // n_ka
    total = own_ref[...]
    for ref in got:
        total = total + ref[...].astype(F32)
    for k in range(n_ka):
        stage_ref[z ^ k, 0:piece, :] = total[k * piece : (k + 1) * piece]
    out_ref[...] = stage_ref[0, 0:piece, :]
    for s, send in enumerate(sends, 1):
        send[...] = stage_ref[s, 0:piece, :].astype(BF16)
    query = gq_ref[...].astype(F32)
    wide = query.shape[0] // rows
    far_ref[...] = jnp.where(core == 0, query[0:wide], query[(rows - 1) * wide :]).astype(BF16)


def combine_kernel(n_ka, *refs):
    own_ref, *got = refs[:n_ka]
    gk_ref, out_ref, *sends, ext_ref = refs[n_ka:]
    _, _, z = place()
    piece = own_ref.shape[0]
    total = own_ref[...]
    for ref in got:
        total = total + ref[...].astype(F32)
    total = total.astype(BF16)
    out_ref[...] = total
    tall, key_rows, _ = ext_ref.shape
    ext_ref[...] = gk_ref[...].astype(F32).reshape(ext_ref.shape)
    first, last = ext_ref[:, 0, :], ext_ref[:, key_rows - 1, :]
    for s, send in enumerate(sends, 1):
        send[0:piece, :] = total
        if joins(s):
            send[piece : piece + tall, :] = jnp.where((z ^ s) == z + 1, last, first).astype(BF16)


def image_kernel(piece, rows, gq_ref, near_ref, far_ref, gk_ref, w_ref, *rest):
    *got, qo_ref, ko_ref, end_ref, qext_ref, kext_ref = rest
    wide, channels = near_ref.shape
    tall = kext_ref.shape[0]
    key_rows = gk_ref.shape[0] // tall
    tile_q = wide - 2
    tile_k = tall - 2
    _, core, z = place()
    near, far = near_ref[...].astype(F32), far_ref[...].astype(F32)
    lines = [(s, ref[piece : piece + tall, :].astype(F32)) for s, ref in enumerate(got, 1) if joins(s)]
    qext_ref[0, 0:wide, :] = jnp.where(core == 0, far, near)
    query = gq_ref[...].astype(F32)
    for row in range(rows):
        qext_ref[row + 1, 0:wide, :] = query[row * wide : (row + 1) * wide]
    qext_ref[rows + 1, 0:wide, :] = jnp.where(core == 0, near, far)
    kext_ref[:, 8 : 8 + key_rows, :] = gk_ref[...].astype(F32).reshape(tall, key_rows, channels)
    kext_ref[:, 7, :] = carried(lines, z, -1)
    kext_ref[:, 8 + key_rows, :] = carried(lines, z, 1)
    total = None
    for tap in range(9):
        a, b = tap // 3 - 1, tap % 3 - 1
        first = qext_ref[1 - a : 1 - a + rows, 1 - b : 1 - b + tile_q, :].reshape(rows * tile_q, channels)
        second = kext_ref[1 - b : 1 - b + tile_k, 8 - a : 8 - a + key_rows, :].reshape(tile_k * key_rows, channels)
        grad = jnp.concatenate([first.astype(BF16), second.astype(BF16)], axis=0)
        part = lax.dot_general(grad, w_ref[tap], (((1,), (1,)), ((), ())), preferred_element_type=F32)
        total = part if total is None else total + part
    count = qo_ref.shape[0]
    qo_ref[...] = total[:count].astype(BF16)
    ko_ref[...] = total[count:].astype(BF16)
    end_ref[...] = jnp.zeros_like(end_ref)


def gather_kernel(count, axis, *refs):
    z = place()[axis]
    *_, out_ref, stage_ref = refs
    piece = refs[0].shape[0]
    for s in range(count):
        stage_ref[z ^ s, 0:piece, :] = refs[s][0:piece, :].astype(F32)
    for k in range(count):
        out_ref[k * piece : (k + 1) * piece, :] = stage_ref[k, 0:piece, :].astype(BF16)


def widen_kernel(other, *refs):
    half_ref, out_hbm, wide_ref, sems = refs[0], *refs[-3:]
    _, core, _ = place()
    half = half_ref.shape[0]
    count = sems.shape[0]
    size = half // count
    base = (1 - core if other else core) * half
    copies = []
    for i in range(count):
        wide_ref[i * size : (i + 1) * size, :] = half_ref[i * size : (i + 1) * size, :].astype(F32)
        rows = pl.ds(pl.multiple_of(base + i * size, 8), size)
        copies.append(pltpu.make_async_copy(wide_ref.at[pl.ds(i * size, size)], out_hbm.at[rows], sems.at[i]))
        copies[-1].start()
    for copy in copies:
        copy.wait()


def widen(half, whole=None):
    rows, channels = half.shape
    hbm = pl.BlockSpec(memory_space=pltpu.HBM)
    vmem = pl.BlockSpec(memory_space=pltpu.VMEM)
    more = [] if whole is None else [pltpu.with_memory_space_constraint(whole, pltpu.HBM)]
    return pl.pallas_call(
        functools.partial(widen_kernel, whole is not None),
        in_specs=[vmem] + [hbm] * len(more),
        out_specs=hbm,
        out_shape=jax.ShapeDtypeStruct((2 * rows, channels), F32),
        scratch_shapes=[pltpu.VMEM((rows, channels), F32), pltpu.SemaphoreType.DMA((4,))],
        input_output_aliases={1: 0} if more else {},
        compiler_params=pltpu.CompilerParams(vmem_limit_bytes=SMALL_BYTES),
        name="widen",
    )(half, *more)


def call(kernel, name, outs, args, scratch=(), after=()):
    return pl.pallas_call(
        kernel,
        in_specs=[pl.BlockSpec(memory_space=pltpu.VMEM)] * len(args) + [pl.BlockSpec(memory_space=pl.ANY)] * len(after),
        out_shape=[jax.ShapeDtypeStruct(shape, dtype) for shape, dtype in outs],
        scratch_shapes=[pltpu.VMEM(shape, F32) for shape in scratch],
        compiler_params=pltpu.CompilerParams(vmem_limit_bytes=SMALL_BYTES),
        name=name,
    )(*args, *after)


def body(query_features, key_features, pyramid_grad, query_image, key_image, conv_weight):
    n_pb = lax.axis_size("pb")
    n_ka = lax.axis_size("ka")
    n_quad = n_pb // 2
    quad, core, z = place()
    strip_rows, width, channels = query_features.shape
    key_rows = key_features.shape[1]
    cin = conv_weight.shape[2]
    tile_q = width // n_ka
    tile_k = width // n_pb
    wide = tile_q + 2
    tall = tile_k + 2
    size = tall * key_rows
    taps = 9
    half = taps * cin // 2
    quarter = half // n_quad
    piece = quarter // n_ka

    def to_core(x):
        return lax.ppermute(x, "pb", flip(n_pb, 1))

    def to_quad(parts):
        return [lax.ppermute(x, "pb", flip(n_pb, 2 * s)) for s, x in enumerate(parts, 1)]

    def to_chip(x):
        links = [(i, i + 1) for i in range(1, n_pb - 1, 2)]
        return lax.ppermute(x, "pb", links + [(d, s) for s, d in links])

    def to_layers(parts):
        return [lax.ppermute(x, "ka", flip(n_ka, s)) for s, x in enumerate(parts, 1)]

    def extra(count, mask, more):
        return count + (more if joins(mask) else 0)

    grads = jnp.transpose(pyramid_grad.reshape(pyramid_grad.shape[0], pyramid_grad.shape[2]))
    *q_parts, k_send, k_keep = correlate(
        grads,
        query_features.reshape(strip_rows * width, channels),
        key_features.reshape(width * key_rows, channels),
        query_image,
        key_image,
        width,
        key_rows,
        n_ka,
        n_quad,
    )
    k_recv = to_core(k_send)
    q_recv = to_layers(q_parts[1:])
    outs = [((size, channels), F32), ((tile_q, cin), BF16)]
    outs += [((extra(size, s, tile_q), channels), BF16) for s in range(1, n_quad)]
    k_own, near, *k_pair = call(functools.partial(pair_kernel, size, tile_q), "pairs", outs, (k_keep, k_recv))
    k_more = to_quad(k_pair)
    outs = [
        ((half + wide, channels), BF16),
        ((half, channels), F32),
        ((strip_rows * wide, channels), BF16),
        ((size, channels), BF16),
    ]
    w_send, w_keep, gq, gk = call(
        functools.partial(weight_kernel, n_ka, n_quad),
        "weights",
        outs,
        (q_parts[0], *q_recv, k_own, *k_more, near, query_image, key_image),
        [(taps * cin, channels), (strip_rows * wide, channels), (tile_k, key_rows + 16, cin)],
    )

    w_recv = to_core(w_send)
    outs = [((quarter, channels), F32), ((wide, channels), BF16)]
    outs += [((quarter, channels), BF16)] * (n_quad - 1)
    own, near, *sends = call(piece_kernel, "pieces", outs, (w_keep, w_recv), [(half, channels)])
    got = to_quad(sends)
    own, far, *sends = call(
        functools.partial(layer_kernel, n_quad, strip_rows),
        "layers",
        [((piece, channels), F32), ((wide, channels), BF16)] + [((piece, channels), BF16)] * (n_ka - 1),
        (own, *got, gq),
        [(n_ka, up16(piece), channels)],
    )
    got = to_layers(sends)
    far = to_chip(far)
    part, *sends = call(
        functools.partial(combine_kernel, n_ka),
        "combine",
        [((piece, channels), BF16)] + [((extra(piece, s, tall), channels), BF16) for s in range(1, n_ka)],
        (own, *got, gk),
        [(tall, key_rows, channels)],
    )
    got = to_layers(sends)
    (part,) = call(
        functools.partial(gather_kernel, n_ka, 2),
        "gather",
        [((quarter, channels), BF16)],
        (part, *got),
        [(n_ka, up16(piece), channels)],
    )
    q_out, k_out, end = call(
        functools.partial(image_kernel, piece, strip_rows),
        "images",
        [((strip_rows * tile_q, cin), BF16), ((tile_k * key_rows, cin), BF16), ((8, 128), F32)],
        (gq, near, far, gk, conv_weight.reshape(taps, cin, channels), *got),
        [(strip_rows + 2, up16(wide), channels), (tall, key_rows + 16, channels)],
    )
    (part,) = call(
        functools.partial(gather_kernel, n_quad, 0),
        "gather",
        [((half, channels), BF16)],
        (part, *to_quad([part] * (n_quad - 1))),
        [(n_quad, up16(quarter), channels)],
        after=(end,),
    )
    weight_grad = widen(to_core(part), widen(part))
    return (
        q_out.reshape(query_image.shape),
        k_out.reshape(key_image.shape),
        weight_grad.reshape(conv_weight.shape),
    )


def solution(mesh):
    placed = (
        P("pb", None, None),
        P(None, "ka", None),
        P("pb", "ka", None),
        P("pb", "ka", None),
        P("pb", "ka", None),
        P(),
    )
    return jax.shard_map(
        body,
        mesh=mesh,
        in_specs=placed,
        out_specs=(P("pb", "ka", None), P("pb", "ka", None), P()),
        check_vma=False,
    )
```

```python
import functools

import jax
import jax.numpy as jnp
from jax import lax
from jax.experimental import pallas as pl
from jax.experimental.pallas import tpu as pltpu
from jax.sharding import PartitionSpec as P

LEVELS = 4
F32 = jnp.float32
BF16 = jnp.bfloat16
SMALL_BYTES = 16 * 2**20


def flip(count, mask):
    return [(i, i ^ mask) for i in range(count)]


def put(ref, rows, value):
    for lane in range(ref.shape[0]):
        ref[lane, rows, :] = value[:, lane * 128 : (lane + 1) * 128]


def get(ref, rows):
    return jnp.concatenate([ref[lane, rows, :] for lane in range(ref.shape[0])], axis=1)


def up16(count):
    return -(-count // 16) * 16


def joins(mask):
    return (mask & (mask + 1)) == 0


def place():
    pb = lax.axis_index("pb")
    return pb // 2, pb % 2, lax.axis_index("ka")


def carried(parts, index, step):
    total = None
    for mask, row in parts:
        row = jnp.where((index ^ mask) == index + step, row, 0.0)
        total = row if total is None else total + row
    return total


def corr_kernel(dims, a_hbm, q_hbm, key_hbm, qi_hbm, ki_hbm, *rest):
    width, key_rows, tile_q, tile_k, n_ka, n_quad, chunk = dims
    q_outs = rest[:n_ka]
    send_ref, keep_ref = rest[n_ka : n_ka + 2]
    a_ref, q_ref, key_ref, cells_ref, coarse_ref, keyf_ref, tmp_ref, kpad_ref, qpad_ref, stage_ref, qi_ref, ki_ref, sems = rest[n_ka + 2 :]
    count, channels = q_ref.shape
    rows = count // width
    scale = channels ** (-0.5)
    quad, core, z = place()

    copies = [pltpu.make_async_copy(key_hbm, key_ref, sems.at[0])]
    for i in range(count // chunk):
        lanes = pl.ds(i * chunk, chunk)
        copies.append(pltpu.make_async_copy(a_hbm.at[:, lanes], a_ref.at[:, lanes], sems.at[i + 2]))
    copies.append(pltpu.make_async_copy(q_hbm, q_ref, sems.at[1]))
    copies.append(pltpu.make_async_copy(qi_hbm, qi_ref, sems.at[count // chunk + 2]))
    copies.append(pltpu.make_async_copy(ki_hbm, ki_ref, sems.at[count // chunk + 3]))
    for copy in copies:
        copy.start()

    qpad_ref[...] = jnp.zeros_like(qpad_ref)
    edge = jnp.zeros((key_rows, channels), F32)
    put(kpad_ref, slice(0, key_rows), edge)
    put(kpad_ref, slice((width + 1) * key_rows, (width + 2) * key_rows), edge)

    copies[0].wait()
    put(keyf_ref, slice(None), key_ref[...].astype(F32))
    lines = [get(keyf_ref, pl.ds(r, width, stride=key_rows)) for r in range(key_rows)]
    offset = 0
    for level in range(LEVELS):
        w = width >> level
        if level:
            pairs = []
            for i in range(len(lines) // 2):
                put(tmp_ref, slice(0, 2 * w), lines[2 * i] + lines[2 * i + 1])
                pairs.append(get(tmp_ref, pl.ds(0, w, stride=2)) + get(tmp_ref, pl.ds(1, w, stride=2)))
            lines = pairs
        for line in lines:
            cells_ref[offset : offset + w, :] = line * (4.0**-level)
            offset += w
    cells = cells_ref[...].astype(BF16)
    for copy in copies[1:]:
        copy.wait()
    query = lax.dot_general(cells, a_ref[...], (((0,), (0,)), ((), ())), preferred_element_type=F32).T * scale

    last_row = ki_ref[...].astype(F32)
    first_row, last_row = last_row[:, 0], last_row[:, key_rows - 1]
    wide = tile_q + 2
    for s in range(1, n_ka):
        if joins(s):
            stage_ref[s, rows * wide : rows * wide + tile_k, :] = jnp.where((z ^ s) == z + 1, last_row, first_row)
    base = n_quad * (tile_k + 2) * key_rows
    send_ref[base : base + tile_q, :] = qi_ref[0]
    send_ref[base + up16(tile_q) : base + up16(tile_q) + tile_q, :] = qi_ref[rows - 1]
    coarse_ref[...] = jnp.dot(a_ref[...], q_ref[...], preferred_element_type=F32)
    for row in range(rows):
        qpad_ref[8 : 8 + width, :] = query[row * width : (row + 1) * width]
        for k in range(n_ka):
            stage_ref[z ^ k, row * wide : (row + 1) * wide, :] = qpad_ref[7 + tile_q * k : 9 + tile_q * (k + 1), :]
    for s in range(n_ka):
        q_outs[s][...] = stage_ref[s, 0 : q_outs[s].shape[0], :].astype(BF16)

    offsets = [0]
    for level in range(LEVELS):
        offsets.append(offsets[-1] + (key_rows >> level) * (width >> level))
    finer = None
    for level in reversed(range(LEVELS)):
        w = width >> level
        here = []
        for r in range(key_rows >> level):
            start = offsets[level] + r * w
            value = coarse_ref[start : start + w, :] * (scale * 4.0**-level)
            if finer is not None:
                value = value + finer[r // 2]
            here.append(value)
        if level:
            finer = []
            for value in here:
                put(tmp_ref, pl.ds(0, w, stride=2), value)
                put(tmp_ref, pl.ds(1, w, stride=2), value)
                finer.append(get(tmp_ref, slice(0, 2 * w)))
    for r in range(key_rows):
        put(kpad_ref, pl.ds(key_rows + r, width, stride=key_rows), here[r])
    size = (tile_k + 2) * key_rows
    for s in range(n_quad):
        first = (quad ^ s) * 2 * tile_k * key_rows
        mine = pl.multiple_of(first + core * tile_k * key_rows, 8)
        other = pl.multiple_of(first + (1 - core) * tile_k * key_rows, 8)
        keep_ref[s] = get(kpad_ref, pl.ds(mine, size))
        send_ref[s * size : (s + 1) * size, :] = get(kpad_ref, pl.ds(other, size)).astype(BF16)


def correlate(grads, queries, keys, query_image, key_image, width, key_rows, n_ka, n_quad):
    cells, count = grads.shape
    channels = queries.shape[1]
    rows = count // width
    tile_q = width // n_ka
    tile_k = width // (2 * n_quad)
    size = (tile_k + 2) * key_rows
    counts = [rows * (tile_q + 2) + (tile_k if s and joins(s) else 0) for s in range(n_ka)]
    chunk = 256
    hbm = pl.BlockSpec(memory_space=pltpu.HBM)
    vmem = pl.BlockSpec(memory_space=pltpu.VMEM)
    dims = (width, key_rows, tile_q, tile_k, n_ka, n_quad, chunk)
    lanes = channels // 128
    return pl.pallas_call(
        functools.partial(corr_kernel, dims),
        in_specs=[hbm] * 5,
        out_specs=[vmem] * (n_ka + 2),
        out_shape=[
            jax.ShapeDtypeStruct((count, channels), BF16) for count in counts
        ]
        + [
            jax.ShapeDtypeStruct((n_quad * size + 2 * up16(tile_q), channels), BF16),
            jax.ShapeDtypeStruct((n_quad, size, channels), F32),
        ],
        scratch_shapes=[
            pltpu.VMEM((cells, count), BF16),
            pltpu.VMEM((count, channels), BF16),
            pltpu.VMEM((width * key_rows, channels), BF16),
            pltpu.VMEM((cells, channels), F32),
            pltpu.VMEM((cells, channels), F32),
            pltpu.VMEM((lanes, width * key_rows, 128), F32),
            pltpu.VMEM((lanes, width, 128), F32),
            pltpu.VMEM((lanes, (width + 2) * key_rows, 128), F32),
            pltpu.VMEM((width + 16, channels), F32),
            pltpu.VMEM((n_ka, up16(max(counts)), channels), F32),
            pltpu.VMEM(query_image.shape, BF16),
            pltpu.VMEM(key_image.shape, BF16),
            pltpu.SemaphoreType.DMA((count // chunk + 4,)),
        ],
        compiler_params=pltpu.CompilerParams(vmem_limit_bytes=cells * (count * 4 + channels * 24)),
        name="correlate",
    )(*[pltpu.with_memory_space_constraint(x, pltpu.HBM) for x in (grads, queries, keys, query_image, key_image)])


def pair_kernel(size, tile, keep_ref, recv_ref, own_ref, near_ref, *sends):
    quad, core, _ = place()
    n_quad = len(sends) + 1
    base = n_quad * size
    first = recv_ref[base : base + tile, :].astype(F32)
    last = recv_ref[base + up16(tile) : base + up16(tile) + tile, :].astype(F32)
    near_ref[...] = jnp.where(core == 0, first, last).astype(BF16)
    onward = jnp.where(core == 0, last, first).astype(BF16)
    own_ref[...] = keep_ref[0] + recv_ref[0:size, :].astype(F32)
    for s, send in enumerate(sends, 1):
        send[0:size, :] = (keep_ref[s] + recv_ref[s * size : (s + 1) * size, :].astype(F32)).astype(BF16)
        if joins(s):
            send[size : size + tile, :] = onward


def both_sides(refs, near_ref, size, quad, core):
    tile = near_ref.shape[0]
    parts = [(s, ref[size : size + tile, :].astype(F32)) for s, ref in enumerate(refs, 1) if joins(s)]
    near = near_ref[...].astype(F32)
    far = carried(parts, quad, 2 * core - 1)
    return jnp.where(core == 0, far, near), jnp.where(core == 0, near, far)


def weight_kernel(n_ka, n_quad, *refs):
    q_refs = refs[:n_ka]
    k_refs = refs[n_ka : n_ka + n_quad]
    near_ref, qi_ref, ki_ref = refs[n_ka + n_quad : n_ka + n_quad + 3]
    send_ref, keep_ref, gq_ref, gk_ref, acc_ref, sum_ref, ext_ref = refs[n_ka + n_quad + 3 :]
    size, channels = gk_ref.shape
    tile_k, key_rows, cin = ki_ref.shape
    rows, tile_q, _ = qi_ref.shape
    wide = tile_q + 2
    quad, core, z = place()
    top, bottom = both_sides(k_refs[1:], near_ref, size, quad, core)
    lines = [(s, ref[rows * wide : rows * wide + tile_k, :].astype(F32)) for s, ref in enumerate(q_refs) if s and joins(s)]
    ext_ref[:, 8 : 8 + key_rows, :] = ki_ref[...].astype(F32)
    ext_ref[:, 7, :] = carried(lines, z, -1)
    ext_ref[:, 8 + key_rows, :] = carried(lines, z, 1)
    query = jnp.concatenate([top[None], qi_ref[...].astype(F32), bottom[None]], axis=0)
    image = []
    for a in (-1, 0, 1):
        first = query[1 + a : 1 + a + rows].reshape(rows * tile_q, cin)
        second = ext_ref[:, 8 + a : 8 + a + key_rows, :].reshape(tile_k * key_rows, cin)
        image.append(jnp.concatenate([first, second], axis=0).T.astype(BF16))
    image = jnp.concatenate(image, axis=0)
    query = q_refs[0][...].astype(F32)
    for ref in q_refs[1:]:
        query = query + ref[0 : rows * wide, :].astype(F32)
    gq = query.astype(BF16)
    gq_ref[...] = gq
    sum_ref[...] = gq.astype(F32)
    key = k_refs[0][...]
    for ref in k_refs[1:]:
        key = key + ref[0:size, :].astype(F32)
    gk = key.astype(BF16)
    gk_ref[...] = gk
    count = tile_k * key_rows
    for b in (-1, 0, 1):
        starts = [row * wide + 1 - b for row in range(rows)]
        first = jnp.concatenate([sum_ref[start : start + tile_q, :] for start in starts], axis=0).astype(BF16)
        grad = jnp.concatenate([first, gk[(1 - b) * key_rows : (1 - b) * key_rows + count]], axis=0)
        part = jnp.dot(image, grad, preferred_element_type=F32)
        for a in range(3):
            tap = a * 3 + b + 1
            acc_ref[tap * cin : (tap + 1) * cin, :] = part[a * cin : (a + 1) * cin]
    half = keep_ref.shape[0]
    keep_ref[...] = acc_ref[pl.ds(pl.multiple_of(core * half, 16), half), :]
    send_ref[0:half, :] = acc_ref[pl.ds(pl.multiple_of((1 - core) * half, 16), half), :].astype(BF16)
    send_ref[half : half + wide, :] = sum_ref[0:wide, :].astype(BF16)
    send_ref[half + up16(wide) : half + up16(wide) + wide, :] = sum_ref[(rows - 1) * wide : rows * wide, :].astype(BF16)


def piece_kernel(keep_ref, recv_ref, own_ref, near_ref, onward_ref, *rest):
    *sends, sum_ref = rest
    quad, core, _ = place()
    half = keep_ref.shape[0]
    size = own_ref.shape[0]
    tile = near_ref.shape[0]
    first = recv_ref[half : half + tile, :].astype(F32)
    last = recv_ref[half + up16(tile) : half + up16(tile) + tile, :].astype(F32)
    near_ref[...] = jnp.where(core == 0, first, last).astype(BF16)
    onward_ref[...] = jnp.where(core == 0, last, first).astype(BF16)
    sum_ref[...] = keep_ref[...] + recv_ref[0:half, :].astype(F32)
    own_ref[...] = sum_ref[pl.ds(pl.multiple_of(quad * size, 16), size), :]
    for s, send in enumerate(sends, 1):
        send[...] = sum_ref[pl.ds(pl.multiple_of((quad ^ s) * size, 16), size), :].astype(BF16)


def layer_kernel(n_quad, *refs):
    own_ref, *got = refs[:n_quad]
    out_ref, *sends, stage_ref = refs[n_quad + 1 :]
    _, _, z = place()
    n_ka = len(sends) + 1
    size = own_ref.shape[0]
    piece = size // n_ka
    total = own_ref[...]
    for ref in got:
        total = total + ref[...].astype(F32)
    for k in range(n_ka):
        stage_ref[z ^ k, 0:piece, :] = total[k * piece : (k + 1) * piece]
    out_ref[...] = stage_ref[0, 0:piece, :]
    for s, send in enumerate(reversed(sends), 1):
        send[...] = stage_ref[s, 0:piece, :].astype(BF16)


def combine_kernel(n_ka, *refs):
    own_ref, *got = refs[:n_ka]
    gk_ref, out_ref, *sends, ext_ref = refs[n_ka:]
    _, _, z = place()
    piece = own_ref.shape[0]
    total = own_ref[...]
    for ref in got:
        total = total + ref[...].astype(F32)
    total = total.astype(BF16)
    out_ref[...] = total
    tall, key_rows, _ = ext_ref.shape
    ext_ref[...] = gk_ref[...].astype(F32).reshape(ext_ref.shape)
    first, last = ext_ref[:, 0, :], ext_ref[:, key_rows - 1, :]
    for s, send in enumerate(reversed(sends), 1):
        send[0:piece, :] = total
        send[piece : piece + tall, :] = jnp.where((z ^ s) == z + 1, last, first).astype(BF16)


def image_kernel(piece, rows, gq_ref, near_ref, far_ref, gk_ref, w_ref, *rest):
    *got, qo_ref, ko_ref, end_ref, qext_ref, kext_ref = rest
    wide, channels = near_ref.shape
    tall = kext_ref.shape[0]
    key_rows = gk_ref.shape[0] // tall
    tile_q = wide - 2
    tile_k = tall - 2
    _, core, z = place()
    near, far = near_ref[...].astype(F32), far_ref[...].astype(F32)
    lines = [(s, ref[piece : piece + tall, :].astype(F32)) for s, ref in enumerate(reversed(got), 1) if joins(s)]
    qext_ref[0, 0:wide, :] = jnp.where(core == 0, far, near)
    query = gq_ref[...].astype(F32)
    for row in range(rows):
        qext_ref[row + 1, 0:wide, :] = query[row * wide : (row + 1) * wide]
    qext_ref[rows + 1, 0:wide, :] = jnp.where(core == 0, near, far)
    kext_ref[:, 8 : 8 + key_rows, :] = gk_ref[...].astype(F32).reshape(tall, key_rows, channels)
    kext_ref[:, 7, :] = carried(lines, z, -1)
    kext_ref[:, 8 + key_rows, :] = carried(lines, z, 1)
    total = None
    for tap in range(9):
        a, b = tap // 3 - 1, tap % 3 - 1
        first = qext_ref[1 - a : 1 - a + rows, 1 - b : 1 - b + tile_q, :].reshape(rows * tile_q, channels)
        second = kext_ref[1 - b : 1 - b + tile_k, 8 - a : 8 - a + key_rows, :].reshape(tile_k * key_rows, channels)
        grad = jnp.concatenate([first.astype(BF16), second.astype(BF16)], axis=0)
        part = lax.dot_general(grad, w_ref[tap], (((1,), (1,)), ((), ())), preferred_element_type=F32)
        total = part if total is None else total + part
    count = qo_ref.shape[0]
    qo_ref[...] = total[:count].astype(BF16)
    ko_ref[...] = total[count:].astype(BF16)
    end_ref[...] = jnp.zeros_like(end_ref)


def gather_kernel(count, axis, *refs):
    own = place()[axis]
    *_, out_ref, stage_ref = refs
    piece = refs[0].shape[0]
    for i in range(count):
        stage_ref[own ^ ((count - i) % count), 0:piece, :] = refs[i][0:piece, :].astype(F32)
    for k in range(count):
        out_ref[k * piece : (k + 1) * piece, :] = stage_ref[k, 0:piece, :].astype(BF16)


def widen_kernel(other, *refs):
    half_ref, out_hbm, wide_ref, sems = refs[0], *refs[-3:]
    _, core, _ = place()
    half = half_ref.shape[0]
    count = sems.shape[0]
    size = half // count
    base = (1 - core if other else core) * half
    copies = []
    for i in range(count):
        wide_ref[i * size : (i + 1) * size, :] = half_ref[i * size : (i + 1) * size, :].astype(F32)
        rows = pl.ds(pl.multiple_of(base + i * size, 8), size)
        copies.append(pltpu.make_async_copy(wide_ref.at[pl.ds(i * size, size)], out_hbm.at[rows], sems.at[i]))
        copies[-1].start()
    for copy in copies:
        copy.wait()


def widen(half, whole=None):
    rows, channels = half.shape
    hbm = pl.BlockSpec(memory_space=pltpu.HBM)
    vmem = pl.BlockSpec(memory_space=pltpu.VMEM)
    more = [] if whole is None else [pltpu.with_memory_space_constraint(whole, pltpu.HBM)]
    return pl.pallas_call(
        functools.partial(widen_kernel, whole is not None),
        in_specs=[vmem] + [hbm] * len(more),
        out_specs=hbm,
        out_shape=jax.ShapeDtypeStruct((2 * rows, channels), F32),
        scratch_shapes=[pltpu.VMEM((rows, channels), F32), pltpu.SemaphoreType.DMA((4,))],
        input_output_aliases={1: 0} if more else {},
        compiler_params=pltpu.CompilerParams(vmem_limit_bytes=SMALL_BYTES),
        name="widen",
    )(half, *more)


def call(kernel, name, outs, args, scratch=(), after=()):
    return pl.pallas_call(
        kernel,
        in_specs=[pl.BlockSpec(memory_space=pltpu.VMEM)] * len(args) + [pl.BlockSpec(memory_space=pl.ANY)] * len(after),
        out_shape=[jax.ShapeDtypeStruct(shape, dtype) for shape, dtype in outs],
        scratch_shapes=[pltpu.VMEM(shape, F32) for shape in scratch],
        compiler_params=pltpu.CompilerParams(vmem_limit_bytes=SMALL_BYTES),
        name=name,
    )(*args, *after)


def body(query_features, key_features, pyramid_grad, query_image, key_image, conv_weight):
    n_pb = lax.axis_size("pb")
    n_ka = lax.axis_size("ka")
    n_quad = n_pb // 2
    quad, core, z = place()
    strip_rows, width, channels = query_features.shape
    key_rows = key_features.shape[1]
    cin = conv_weight.shape[2]
    tile_q = width // n_ka
    tile_k = width // n_pb
    wide = tile_q + 2
    tall = tile_k + 2
    size = tall * key_rows
    taps = 9
    half = taps * cin // 2
    quarter = half // n_quad
    piece = quarter // n_ka

    def to_core(x):
        return lax.ppermute(x, "pb", flip(n_pb, 1))

    def to_quad(parts):
        return [lax.ppermute(x, "pb", flip(n_pb, 2 * s)) for s, x in enumerate(parts, 1)]

    def to_layers(parts):
        return [lax.ppermute(x, "ka", flip(n_ka, s)) for s, x in enumerate(parts, 1)]

    def to_far_layers(parts):
        return [lax.ppermute(x, "ka", flip(n_ka, n_ka - i)) for i, x in enumerate(parts, 1)]

    def extra(count, mask, more):
        return count + (more if joins(mask) else 0)

    grads = jnp.transpose(pyramid_grad.reshape(pyramid_grad.shape[0], pyramid_grad.shape[2]))
    *q_parts, k_send, k_keep = correlate(
        grads,
        query_features.reshape(strip_rows * width, channels),
        key_features.reshape(width * key_rows, channels),
        query_image,
        key_image,
        width,
        key_rows,
        n_ka,
        n_quad,
    )
    k_recv = to_core(k_send)
    q_recv = to_layers(q_parts[1:])
    outs = [((size, channels), F32), ((tile_q, cin), BF16)]
    outs += [((extra(size, s, tile_q), channels), BF16) for s in range(1, n_quad)]
    k_own, near, *k_pair = call(functools.partial(pair_kernel, size, tile_q), "pairs", outs, (k_keep, k_recv))
    k_more = to_quad(k_pair)
    outs = [
        ((half + 2 * up16(wide), channels), BF16),
        ((half, channels), F32),
        ((strip_rows * wide, channels), BF16),
        ((size, channels), BF16),
    ]
    w_send, w_keep, gq, gk = call(
        functools.partial(weight_kernel, n_ka, n_quad),
        "weights",
        outs,
        (q_parts[0], *q_recv, k_own, *k_more, near, query_image, key_image),
        [(taps * cin, channels), (strip_rows * wide, channels), (tile_k, key_rows + 16, cin)],
    )

    w_recv = to_core(w_send)
    outs = [((quarter, channels), F32)] + [((wide, channels), BF16)] * 2 + [((quarter, channels), BF16)] * (n_quad - 1)
    own, near, far, *sends = call(piece_kernel, "pieces", outs, (w_keep, w_recv), [(half, channels)])
    got = to_quad(sends)
    firsts = range(0, n_pb - 2, 2)
    far = lax.ppermute(far, "pb", [(i, i + 2) for i in firsts] + [(i + 3, i + 1) for i in firsts])
    own, *sends = call(
        functools.partial(layer_kernel, n_quad),
        "layers",
        [((piece, channels), F32)] + [((piece, channels), BF16)] * (n_ka - 1),
        (own, *got),
        [(n_ka, up16(piece), channels)],
        after=(far,),
    )
    got = to_far_layers(sends)
    part, *sends = call(
        functools.partial(combine_kernel, n_ka),
        "combine",
        [((piece, channels), BF16)] + [((piece + tall, channels), BF16)] * (n_ka - 1),
        (own, *got, gk),
        [(tall, key_rows, channels)],
    )
    got = to_far_layers(sends)
    (part,) = call(
        functools.partial(gather_kernel, n_ka, 2),
        "gather",
        [((quarter, channels), BF16)],
        (part, *got),
        [(n_ka, up16(piece), channels)],
    )
    q_out, k_out, end = call(
        functools.partial(image_kernel, piece, strip_rows),
        "images",
        [((strip_rows * tile_q, cin), BF16), ((tile_k * key_rows, cin), BF16), ((8, 128), F32)],
        (gq, near, far, gk, conv_weight.reshape(taps, cin, channels), *got),
        [(strip_rows + 2, up16(wide), channels), (tall, key_rows + 16, channels)],
    )
    (part,) = call(
        functools.partial(gather_kernel, n_quad, 0),
        "gather",
        [((half, channels), BF16)],
        (part, *reversed(to_quad([part] * (n_quad - 1)))),
        [(n_quad, up16(quarter), channels)],
        after=(end,),
    )
    weight_grad = widen(to_core(part), widen(part))
    return (
        q_out.reshape(query_image.shape),
        k_out.reshape(key_image.shape),
        weight_grad.reshape(conv_weight.shape),
    )


def solution(mesh):
    placed = (
        P("pb", None, None),
        P(None, "ka", None),
        P("pb", "ka", None),
        P("pb", "ka", None),
        P("pb", "ka", None),
        P(),
    )
    return jax.shard_map(
        body,
        mesh=mesh,
        in_specs=placed,
        out_specs=(P("pb", "ka", None), P("pb", "ka", None), P()),
        check_vma=False,
    )
```

```python
import functools

import jax
import jax.numpy as jnp
from jax import lax
from jax.experimental import pallas as pl
from jax.experimental.pallas import tpu as pltpu
from jax.sharding import PartitionSpec as P

LEVELS = 4
F32 = jnp.float32
BF16 = jnp.bfloat16
SMALL_BYTES = 16 * 2**20


def flip(count, mask):
    return [(i, i ^ mask) for i in range(count)]


def put(ref, rows, value):
    for lane in range(ref.shape[0]):
        ref[lane, rows, :] = value[:, lane * 128 : (lane + 1) * 128]


def get(ref, rows):
    return jnp.concatenate([ref[lane, rows, :] for lane in range(ref.shape[0])], axis=1)


def up16(count):
    return -(-count // 16) * 16


def joins(mask):
    return (mask & (mask + 1)) == 0


def place():
    pb = lax.axis_index("pb")
    return pb // 2, pb % 2, lax.axis_index("ka")


def carried(parts, index, step):
    total = None
    for mask, row in parts:
        row = jnp.where((index ^ mask) == index + step, row, 0.0)
        total = row if total is None else total + row
    return total


def corr_kernel(dims, a_hbm, q_hbm, key_hbm, qi_hbm, ki_hbm, *rest):
    width, key_rows, tile_q, tile_k, n_ka, n_quad, chunk = dims
    q_outs = rest[:n_ka]
    send_ref, keep_ref = rest[n_ka : n_ka + 2]
    a_ref, q_ref, key_ref, cells_ref, coarse_ref, keyf_ref, tmp_ref, kpad_ref, qpad_ref, stage_ref, qi_ref, ki_ref, sems = rest[n_ka + 2 :]
    count, channels = q_ref.shape
    rows = count // width
    scale = channels ** (-0.5)
    quad, core, z = place()

    copies = [pltpu.make_async_copy(key_hbm, key_ref, sems.at[0])]
    for i in range(count // chunk):
        lanes = pl.ds(i * chunk, chunk)
        copies.append(pltpu.make_async_copy(a_hbm.at[:, lanes], a_ref.at[:, lanes], sems.at[i + 2]))
    copies.append(pltpu.make_async_copy(q_hbm, q_ref, sems.at[1]))
    copies.append(pltpu.make_async_copy(qi_hbm, qi_ref, sems.at[count // chunk + 2]))
    copies.append(pltpu.make_async_copy(ki_hbm, ki_ref, sems.at[count // chunk + 3]))
    for copy in copies:
        copy.start()

    qpad_ref[...] = jnp.zeros_like(qpad_ref)
    edge = jnp.zeros((key_rows, channels), F32)
    put(kpad_ref, slice(0, key_rows), edge)
    put(kpad_ref, slice((width + 1) * key_rows, (width + 2) * key_rows), edge)

    copies[0].wait()
    put(keyf_ref, slice(None), key_ref[...].astype(F32))
    lines = [get(keyf_ref, pl.ds(r, width, stride=key_rows)) for r in range(key_rows)]
    offset = 0
    for level in range(LEVELS):
        w = width >> level
        if level:
            pairs = []
            for i in range(len(lines) // 2):
                put(tmp_ref, slice(0, 2 * w), lines[2 * i] + lines[2 * i + 1])
                pairs.append(get(tmp_ref, pl.ds(0, w, stride=2)) + get(tmp_ref, pl.ds(1, w, stride=2)))
            lines = pairs
        for line in lines:
            cells_ref[offset : offset + w, :] = line * (4.0**-level)
            offset += w
    cells = cells_ref[...].astype(BF16)
    for copy in copies[1:]:
        copy.wait()
    query = lax.dot_general(cells, a_ref[...], (((0,), (0,)), ((), ())), preferred_element_type=F32).T * scale

    last_row = ki_ref[...].astype(F32)
    first_row, last_row = last_row[:, 0], last_row[:, key_rows - 1]
    wide = tile_q + 2
    for s in range(1, n_ka):
        if joins(s):
            stage_ref[s, rows * wide : rows * wide + tile_k, :] = jnp.where((z ^ s) == z + 1, last_row, first_row)
    base = n_quad * (tile_k + 2) * key_rows
    send_ref[base : base + tile_q, :] = qi_ref[0]
    send_ref[base + up16(tile_q) : base + up16(tile_q) + tile_q, :] = qi_ref[rows - 1]
    coarse_ref[...] = jnp.dot(a_ref[...], q_ref[...], preferred_element_type=F32)
    for row in range(rows):
        qpad_ref[8 : 8 + width, :] = query[row * width : (row + 1) * width]
        for k in range(n_ka):
            stage_ref[z ^ k, row * wide : (row + 1) * wide, :] = qpad_ref[7 + tile_q * k : 9 + tile_q * (k + 1), :]
    for s in range(n_ka):
        q_outs[s][...] = stage_ref[s, 0 : q_outs[s].shape[0], :].astype(BF16)

    offsets = [0]
    for level in range(LEVELS):
        offsets.append(offsets[-1] + (key_rows >> level) * (width >> level))
    finer = None
    for level in reversed(range(LEVELS)):
        w = width >> level
        here = []
        for r in range(key_rows >> level):
            start = offsets[level] + r * w
            value = coarse_ref[start : start + w, :] * (scale * 4.0**-level)
            if finer is not None:
                value = value + finer[r // 2]
            here.append(value)
        if level:
            finer = []
            for value in here:
                put(tmp_ref, pl.ds(0, w, stride=2), value)
                put(tmp_ref, pl.ds(1, w, stride=2), value)
                finer.append(get(tmp_ref, slice(0, 2 * w)))
    for r in range(key_rows):
        put(kpad_ref, pl.ds(key_rows + r, width, stride=key_rows), here[r])
    size = (tile_k + 2) * key_rows
    for s in range(n_quad):
        first = (quad ^ s) * 2 * tile_k * key_rows
        mine = pl.multiple_of(first + core * tile_k * key_rows, 8)
        other = pl.multiple_of(first + (1 - core) * tile_k * key_rows, 8)
        keep_ref[s] = get(kpad_ref, pl.ds(mine, size))
        send_ref[s * size : (s + 1) * size, :] = get(kpad_ref, pl.ds(other, size)).astype(BF16)


def correlate(grads, queries, keys, query_image, key_image, width, key_rows, n_ka, n_quad):
    cells, count = grads.shape
    channels = queries.shape[1]
    rows = count // width
    tile_q = width // n_ka
    tile_k = width // (2 * n_quad)
    size = (tile_k + 2) * key_rows
    counts = [rows * (tile_q + 2) + (tile_k if s and joins(s) else 0) for s in range(n_ka)]
    chunk = 256
    hbm = pl.BlockSpec(memory_space=pltpu.HBM)
    vmem = pl.BlockSpec(memory_space=pltpu.VMEM)
    dims = (width, key_rows, tile_q, tile_k, n_ka, n_quad, chunk)
    lanes = channels // 128
    return pl.pallas_call(
        functools.partial(corr_kernel, dims),
        in_specs=[hbm] * 5,
        out_specs=[vmem] * (n_ka + 2),
        out_shape=[
            jax.ShapeDtypeStruct((count, channels), BF16) for count in counts
        ]
        + [
            jax.ShapeDtypeStruct((n_quad * size + 2 * up16(tile_q), channels), BF16),
            jax.ShapeDtypeStruct((n_quad, size, channels), F32),
        ],
        scratch_shapes=[
            pltpu.VMEM((cells, count), BF16),
            pltpu.VMEM((count, channels), BF16),
            pltpu.VMEM((width * key_rows, channels), BF16),
            pltpu.VMEM((cells, channels), F32),
            pltpu.VMEM((cells, channels), F32),
            pltpu.VMEM((lanes, width * key_rows, 128), F32),
            pltpu.VMEM((lanes, width, 128), F32),
            pltpu.VMEM((lanes, (width + 2) * key_rows, 128), F32),
            pltpu.VMEM((width + 16, channels), F32),
            pltpu.VMEM((n_ka, up16(max(counts)), channels), F32),
            pltpu.VMEM(query_image.shape, BF16),
            pltpu.VMEM(key_image.shape, BF16),
            pltpu.SemaphoreType.DMA((count // chunk + 4,)),
        ],
        compiler_params=pltpu.CompilerParams(vmem_limit_bytes=cells * (count * 4 + channels * 24)),
        name="correlate",
    )(*[pltpu.with_memory_space_constraint(x, pltpu.HBM) for x in (grads, queries, keys, query_image, key_image)])


def pair_kernel(size, tile, keep_ref, recv_ref, own_ref, near_ref, *sends):
    quad, core, _ = place()
    n_quad = len(sends) + 1
    base = n_quad * size
    first = recv_ref[base : base + tile, :].astype(F32)
    last = recv_ref[base + up16(tile) : base + up16(tile) + tile, :].astype(F32)
    near_ref[...] = jnp.where(core == 0, first, last).astype(BF16)
    onward = jnp.where(core == 0, last, first).astype(BF16)
    own_ref[...] = keep_ref[0] + recv_ref[0:size, :].astype(F32)
    for s, send in enumerate(sends, 1):
        send[0:size, :] = (keep_ref[s] + recv_ref[s * size : (s + 1) * size, :].astype(F32)).astype(BF16)
        if joins(s):
            send[size : size + tile, :] = onward


def both_sides(refs, near_ref, size, quad, core):
    tile = near_ref.shape[0]
    parts = [(s, ref[size : size + tile, :].astype(F32)) for s, ref in enumerate(refs, 1) if joins(s)]
    near = near_ref[...].astype(F32)
    far = carried(parts, quad, 2 * core - 1)
    return jnp.where(core == 0, far, near), jnp.where(core == 0, near, far)


def weight_kernel(n_ka, n_quad, *refs):
    q_refs = refs[:n_ka]
    k_refs = refs[n_ka : n_ka + n_quad]
    near_ref, qi_ref, ki_ref = refs[n_ka + n_quad : n_ka + n_quad + 3]
    send_ref, late_ref, keep_ref, gq_ref, gk_ref, acc_ref, sum_ref, ext_ref = refs[n_ka + n_quad + 3 :]
    size, channels = gk_ref.shape
    tile_k, key_rows, cin = ki_ref.shape
    rows, tile_q, _ = qi_ref.shape
    wide = tile_q + 2
    quad, core, z = place()
    top, bottom = both_sides(k_refs[1:], near_ref, size, quad, core)
    lines = [(s, ref[rows * wide : rows * wide + tile_k, :].astype(F32)) for s, ref in enumerate(q_refs) if s and joins(s)]
    ext_ref[:, 8 : 8 + key_rows, :] = ki_ref[...].astype(F32)
    ext_ref[:, 7, :] = carried(lines, z, -1)
    ext_ref[:, 8 + key_rows, :] = carried(lines, z, 1)
    query = jnp.concatenate([top[None], qi_ref[...].astype(F32), bottom[None]], axis=0)
    image = []
    for a in (-1, 0, 1):
        first = query[1 + a : 1 + a + rows].reshape(rows * tile_q, cin)
        second = ext_ref[:, 8 + a : 8 + a + key_rows, :].reshape(tile_k * key_rows, cin)
        image.append(jnp.concatenate([first, second], axis=0).T.astype(BF16))
    image = jnp.concatenate(image, axis=0)
    query = q_refs[0][...].astype(F32)
    for ref in q_refs[1:]:
        query = query + ref[0 : rows * wide, :].astype(F32)
    gq = query.astype(BF16)
    gq_ref[...] = gq
    sum_ref[...] = gq.astype(F32)
    key = k_refs[0][...]
    for ref in k_refs[1:]:
        key = key + ref[0:size, :].astype(F32)
    gk = key.astype(BF16)
    gk_ref[...] = gk
    count = tile_k * key_rows
    for b in (-1, 0, 1):
        starts = [row * wide + 1 - b for row in range(rows)]
        first = jnp.concatenate([sum_ref[start : start + tile_q, :] for start in starts], axis=0).astype(BF16)
        grad = jnp.concatenate([first, gk[(1 - b) * key_rows : (1 - b) * key_rows + count]], axis=0)
        part = jnp.dot(image, grad, preferred_element_type=F32)
        for a in range(3):
            tap = a * 3 + b + 1
            acc_ref[tap * cin : (tap + 1) * cin, :] = part[a * cin : (a + 1) * cin]
    quarter = late_ref.shape[0]
    half = n_quad * quarter
    for s in range(n_quad):
        mine = pl.multiple_of(core * half + (quad ^ s) * quarter, 16)
        other = pl.multiple_of((1 - core) * half + (quad ^ s) * quarter, 16)
        keep_ref[s * quarter : (s + 1) * quarter, :] = acc_ref[pl.ds(mine, quarter), :]
        if s:
            send_ref[(s - 1) * quarter : s * quarter, :] = acc_ref[pl.ds(other, quarter), :].astype(BF16)
        else:
            late_ref[...] = acc_ref[pl.ds(other, quarter), :].astype(BF16)
    base = half - quarter
    send_ref[base : base + wide, :] = sum_ref[0:wide, :].astype(BF16)
    send_ref[base + up16(wide) : base + up16(wide) + wide, :] = sum_ref[(rows - 1) * wide : rows * wide, :].astype(BF16)


def piece_kernel(keep_ref, recv_ref, near_ref, onward_ref, *sends):
    _, core, _ = place()
    size = sends[0].shape[0]
    tile = near_ref.shape[0]
    base = len(sends) * size
    first = recv_ref[base : base + tile, :].astype(F32)
    last = recv_ref[base + up16(tile) : base + up16(tile) + tile, :].astype(F32)
    near_ref[...] = jnp.where(core == 0, first, last).astype(BF16)
    onward_ref[...] = jnp.where(core == 0, last, first).astype(BF16)
    for s, send in enumerate(sends, 1):
        send[...] = (keep_ref[s * size : (s + 1) * size, :] + recv_ref[(s - 1) * size : s * size, :].astype(F32)).astype(BF16)


def layer_kernel(n_quad, *refs):
    keep_ref, *got = refs[: n_quad + 1]
    out_ref, *sends, stage_ref = refs[n_quad + 2 :]
    _, _, z = place()
    n_ka = len(sends) + 1
    size = got[0].shape[0]
    piece = size // n_ka
    total = keep_ref[0:size, :]
    for ref in got:
        total = total + ref[...].astype(F32)
    for k in range(n_ka):
        stage_ref[z ^ k, 0:piece, :] = total[k * piece : (k + 1) * piece]
    out_ref[...] = stage_ref[0, 0:piece, :]
    for s, send in enumerate(reversed(sends), 1):
        send[...] = stage_ref[s, 0:piece, :].astype(BF16)


def combine_kernel(n_ka, *refs):
    own_ref, *got = refs[:n_ka]
    gk_ref, out_ref, *sends, ext_ref = refs[n_ka:]
    _, _, z = place()
    piece = own_ref.shape[0]
    total = own_ref[...]
    for ref in got:
        total = total + ref[...].astype(F32)
    total = total.astype(BF16)
    out_ref[...] = total
    tall, key_rows, _ = ext_ref.shape
    ext_ref[...] = gk_ref[...].astype(F32).reshape(ext_ref.shape)
    first, last = ext_ref[:, 0, :], ext_ref[:, key_rows - 1, :]
    for s, send in enumerate(reversed(sends), 1):
        send[0:piece, :] = total
        send[piece : piece + tall, :] = jnp.where((z ^ s) == z + 1, last, first).astype(BF16)


def image_kernel(piece, rows, gq_ref, near_ref, far_ref, gk_ref, w_ref, *rest):
    *got, qo_ref, ko_ref, end_ref, qext_ref, kext_ref = rest
    wide, channels = near_ref.shape
    tall = kext_ref.shape[0]
    key_rows = gk_ref.shape[0] // tall
    tile_q = wide - 2
    tile_k = tall - 2
    _, core, z = place()
    near, far = near_ref[...].astype(F32), far_ref[...].astype(F32)
    lines = [(s, ref[piece : piece + tall, :].astype(F32)) for s, ref in enumerate(reversed(got), 1) if joins(s)]
    qext_ref[0, 0:wide, :] = jnp.where(core == 0, far, near)
    query = gq_ref[...].astype(F32)
    for row in range(rows):
        qext_ref[row + 1, 0:wide, :] = query[row * wide : (row + 1) * wide]
    qext_ref[rows + 1, 0:wide, :] = jnp.where(core == 0, near, far)
    kext_ref[:, 8 : 8 + key_rows, :] = gk_ref[...].astype(F32).reshape(tall, key_rows, channels)
    kext_ref[:, 7, :] = carried(lines, z, -1)
    kext_ref[:, 8 + key_rows, :] = carried(lines, z, 1)
    total = None
    for tap in range(9):
        a, b = tap // 3 - 1, tap % 3 - 1
        first = qext_ref[1 - a : 1 - a + rows, 1 - b : 1 - b + tile_q, :].reshape(rows * tile_q, channels)
        second = kext_ref[1 - b : 1 - b + tile_k, 8 - a : 8 - a + key_rows, :].reshape(tile_k * key_rows, channels)
        grad = jnp.concatenate([first.astype(BF16), second.astype(BF16)], axis=0)
        part = lax.dot_general(grad, w_ref[tap], (((1,), (1,)), ((), ())), preferred_element_type=F32)
        total = part if total is None else total + part
    count = qo_ref.shape[0]
    qo_ref[...] = total[:count].astype(BF16)
    ko_ref[...] = total[count:].astype(BF16)
    end_ref[...] = jnp.zeros_like(end_ref)


def gather_kernel(count, axis, *refs):
    own = place()[axis]
    *_, out_ref, stage_ref = refs
    piece = refs[0].shape[0]
    for i in range(count):
        stage_ref[own ^ ((count - i) % count), 0:piece, :] = refs[i][0:piece, :].astype(F32)
    for k in range(count):
        out_ref[k * piece : (k + 1) * piece, :] = stage_ref[k, 0:piece, :].astype(BF16)


def widen_kernel(other, *refs):
    half_ref, out_hbm, wide_ref, sems = refs[0], *refs[-3:]
    _, core, _ = place()
    half = half_ref.shape[0]
    count = sems.shape[0]
    size = half // count
    base = (1 - core if other else core) * half
    copies = []
    for i in range(count):
        wide_ref[i * size : (i + 1) * size, :] = half_ref[i * size : (i + 1) * size, :].astype(F32)
        rows = pl.ds(pl.multiple_of(base + i * size, 8), size)
        copies.append(pltpu.make_async_copy(wide_ref.at[pl.ds(i * size, size)], out_hbm.at[rows], sems.at[i]))
        copies[-1].start()
    for copy in copies:
        copy.wait()


def widen(half, whole=None):
    rows, channels = half.shape
    hbm = pl.BlockSpec(memory_space=pltpu.HBM)
    vmem = pl.BlockSpec(memory_space=pltpu.VMEM)
    more = [] if whole is None else [pltpu.with_memory_space_constraint(whole, pltpu.HBM)]
    return pl.pallas_call(
        functools.partial(widen_kernel, whole is not None),
        in_specs=[vmem] + [hbm] * len(more),
        out_specs=hbm,
        out_shape=jax.ShapeDtypeStruct((2 * rows, channels), F32),
        scratch_shapes=[pltpu.VMEM((rows, channels), F32), pltpu.SemaphoreType.DMA((4,))],
        input_output_aliases={1: 0} if more else {},
        compiler_params=pltpu.CompilerParams(vmem_limit_bytes=SMALL_BYTES),
        name="widen",
    )(half, *more)


def call(kernel, name, outs, args, scratch=(), after=()):
    return pl.pallas_call(
        kernel,
        in_specs=[pl.BlockSpec(memory_space=pltpu.VMEM)] * len(args) + [pl.BlockSpec(memory_space=pl.ANY)] * len(after),
        out_shape=[jax.ShapeDtypeStruct(shape, dtype) for shape, dtype in outs],
        scratch_shapes=[pltpu.VMEM(shape, F32) for shape in scratch],
        compiler_params=pltpu.CompilerParams(vmem_limit_bytes=SMALL_BYTES),
        name=name,
    )(*args, *after)


def body(query_features, key_features, pyramid_grad, query_image, key_image, conv_weight):
    n_pb = lax.axis_size("pb")
    n_ka = lax.axis_size("ka")
    n_quad = n_pb // 2
    quad, core, z = place()
    strip_rows, width, channels = query_features.shape
    key_rows = key_features.shape[1]
    cin = conv_weight.shape[2]
    tile_q = width // n_ka
    tile_k = width // n_pb
    wide = tile_q + 2
    tall = tile_k + 2
    size = tall * key_rows
    taps = 9
    half = taps * cin // 2
    quarter = half // n_quad
    piece = quarter // n_ka

    def to_core(x):
        return lax.ppermute(x, "pb", flip(n_pb, 1))

    def to_quad(parts):
        return [lax.ppermute(x, "pb", flip(n_pb, 2 * s)) for s, x in enumerate(parts, 1)]

    def to_layers(parts):
        return [lax.ppermute(x, "ka", flip(n_ka, s)) for s, x in enumerate(parts, 1)]

    def to_far_layers(parts):
        return [lax.ppermute(x, "ka", flip(n_ka, n_ka - i)) for i, x in enumerate(parts, 1)]

    def extra(count, mask, more):
        return count + (more if joins(mask) else 0)

    grads = jnp.transpose(pyramid_grad.reshape(pyramid_grad.shape[0], pyramid_grad.shape[2]))
    *q_parts, k_send, k_keep = correlate(
        grads,
        query_features.reshape(strip_rows * width, channels),
        key_features.reshape(width * key_rows, channels),
        query_image,
        key_image,
        width,
        key_rows,
        n_ka,
        n_quad,
    )
    k_recv = to_core(k_send)
    q_recv = to_layers(q_parts[1:])
    outs = [((size, channels), F32), ((tile_q, cin), BF16)]
    outs += [((extra(size, s, tile_q), channels), BF16) for s in range(1, n_quad)]
    k_own, near, *k_pair = call(functools.partial(pair_kernel, size, tile_q), "pairs", outs, (k_keep, k_recv))
    k_more = to_quad(k_pair)
    outs = [
        ((half - quarter + 2 * up16(wide), channels), BF16),
        ((quarter, channels), BF16),
        ((half, channels), F32),
        ((strip_rows * wide, channels), BF16),
        ((size, channels), BF16),
    ]
    w_send, w_late, w_keep, gq, gk = call(
        functools.partial(weight_kernel, n_ka, n_quad),
        "weights",
        outs,
        (q_parts[0], *q_recv, k_own, *k_more, near, query_image, key_image),
        [(taps * cin, channels), (strip_rows * wide, channels), (tile_k, key_rows + 16, cin)],
    )

    w_recv = to_core(w_send)
    w_late = to_core(w_late)
    outs = [((wide, channels), BF16)] * 2 + [((quarter, channels), BF16)] * (n_quad - 1)
    near, far, *sends = call(piece_kernel, "pieces", outs, (w_keep, w_recv))
    got = to_quad(sends)
    firsts = range(0, n_pb - 2, 2)
    far = lax.ppermute(far, "pb", [(i, i + 2) for i in firsts] + [(i + 3, i + 1) for i in firsts])
    own, *sends = call(
        functools.partial(layer_kernel, n_quad),
        "layers",
        [((piece, channels), F32)] + [((piece, channels), BF16)] * (n_ka - 1),
        (w_keep, w_late, *got),
        [(n_ka, up16(piece), channels)],
        after=(far,),
    )
    got = to_far_layers(sends)
    part, *sends = call(
        functools.partial(combine_kernel, n_ka),
        "combine",
        [((piece, channels), BF16)] + [((piece + tall, channels), BF16)] * (n_ka - 1),
        (own, *got, gk),
        [(tall, key_rows, channels)],
    )
    got = to_far_layers(sends)
    (part,) = call(
        functools.partial(gather_kernel, n_ka, 2),
        "gather",
        [((quarter, channels), BF16)],
        (part, *got),
        [(n_ka, up16(piece), channels)],
    )
    q_out, k_out, end = call(
        functools.partial(image_kernel, piece, strip_rows),
        "images",
        [((strip_rows * tile_q, cin), BF16), ((tile_k * key_rows, cin), BF16), ((8, 128), F32)],
        (gq, near, far, gk, conv_weight.reshape(taps, cin, channels), *got),
        [(strip_rows + 2, up16(wide), channels), (tall, key_rows + 16, channels)],
    )
    (part,) = call(
        functools.partial(gather_kernel, n_quad, 0),
        "gather",
        [((half, channels), BF16)],
        (part, *reversed(to_quad([part] * (n_quad - 1)))),
        [(n_quad, up16(quarter), channels)],
        after=(end,),
    )
    weight_grad = widen(to_core(part), widen(part))
    return (
        q_out.reshape(query_image.shape),
        k_out.reshape(key_image.shape),
        weight_grad.reshape(conv_weight.shape),
    )


def solution(mesh):
    placed = (
        P("pb", None, None),
        P(None, "ka", None),
        P("pb", "ka", None),
        P("pb", "ka", None),
        P("pb", "ka", None),
        P(),
    )
    return jax.shard_map(
        body,
        mesh=mesh,
        in_specs=placed,
        out_specs=(P("pb", "ka", None), P("pb", "ka", None), P()),
        check_vma=False,
    )
```

```python
import functools

import jax
import jax.numpy as jnp
from jax import lax
from jax.experimental import pallas as pl
from jax.experimental.pallas import tpu as pltpu
from jax.sharding import PartitionSpec as P

LEVELS = 4
F32 = jnp.float32
BF16 = jnp.bfloat16
SMALL_BYTES = 16 * 2**20


def flip(count, mask):
    return [(i, i ^ mask) for i in range(count)]


def put(ref, rows, value):
    for lane in range(ref.shape[0]):
        ref[lane, rows, :] = value[:, lane * 128 : (lane + 1) * 128]


def get(ref, rows):
    return jnp.concatenate([ref[lane, rows, :] for lane in range(ref.shape[0])], axis=1)


def up16(count):
    return -(-count // 16) * 16


def joins(mask):
    return (mask & (mask + 1)) == 0


def place():
    pb = lax.axis_index("pb")
    return pb // 2, pb % 2, lax.axis_index("ka")


def carried(parts, index, step):
    total = None
    for mask, row in parts:
        row = jnp.where((index ^ mask) == index + step, row, 0.0)
        total = row if total is None else total + row
    return total


def corr_kernel(dims, a_hbm, q_hbm, key_hbm, qi_hbm, ki_hbm, *rest):
    width, key_rows, tile_q, tile_k, n_ka, n_quad, chunk = dims
    q_outs = rest[:n_ka]
    send_ref, keep_ref = rest[n_ka : n_ka + 2]
    a_ref, q_ref, key_ref, cells_ref, coarse_ref, keyf_ref, tmp_ref, kpad_ref, qpad_ref, stage_ref, qi_ref, ki_ref, sems = rest[n_ka + 2 :]
    count, channels = q_ref.shape
    rows = count // width
    scale = channels ** (-0.5)
    quad, core, z = place()

    copies = [pltpu.make_async_copy(key_hbm, key_ref, sems.at[0])]
    for i in range(count // chunk):
        lanes = pl.ds(i * chunk, chunk)
        copies.append(pltpu.make_async_copy(a_hbm.at[:, lanes], a_ref.at[:, lanes], sems.at[i + 2]))
    copies.append(pltpu.make_async_copy(q_hbm, q_ref, sems.at[1]))
    copies.append(pltpu.make_async_copy(qi_hbm, qi_ref, sems.at[count // chunk + 2]))
    copies.append(pltpu.make_async_copy(ki_hbm, ki_ref, sems.at[count // chunk + 3]))
    for copy in copies:
        copy.start()

    qpad_ref[...] = jnp.zeros_like(qpad_ref)
    edge = jnp.zeros((key_rows, channels), F32)
    put(kpad_ref, slice(0, key_rows), edge)
    put(kpad_ref, slice((width + 1) * key_rows, (width + 2) * key_rows), edge)

    copies[0].wait()
    put(keyf_ref, slice(None), key_ref[...].astype(F32))
    lines = [get(keyf_ref, pl.ds(r, width, stride=key_rows)) for r in range(key_rows)]
    offset = 0
    for level in range(LEVELS):
        w = width >> level
        if level:
            pairs = []
            for i in range(len(lines) // 2):
                put(tmp_ref, slice(0, 2 * w), lines[2 * i] + lines[2 * i + 1])
                pairs.append(get(tmp_ref, pl.ds(0, w, stride=2)) + get(tmp_ref, pl.ds(1, w, stride=2)))
            lines = pairs
        for line in lines:
            cells_ref[offset : offset + w, :] = line * (4.0**-level)
            offset += w
    cells = cells_ref[...].astype(BF16)
    for copy in copies[1:]:
        copy.wait()
    query = lax.dot_general(cells, a_ref[...], (((0,), (0,)), ((), ())), preferred_element_type=F32).T * scale

    last_row = ki_ref[...].astype(F32)
    first_row, last_row = last_row[:, 0], last_row[:, key_rows - 1]
    wide = tile_q + 2
    for s in range(1, n_ka):
        if joins(s):
            stage_ref[s, rows * wide : rows * wide + tile_k, :] = jnp.where((z ^ s) == z + 1, last_row, first_row)
    base = n_quad * (tile_k + 2) * key_rows
    send_ref[base : base + tile_q, :] = qi_ref[0]
    send_ref[base + up16(tile_q) : base + up16(tile_q) + tile_q, :] = qi_ref[rows - 1]
    coarse_ref[...] = jnp.dot(a_ref[...], q_ref[...], preferred_element_type=F32)
    for row in range(rows):
        qpad_ref[8 : 8 + width, :] = query[row * width : (row + 1) * width]
        for k in range(n_ka):
            stage_ref[z ^ k, row * wide : (row + 1) * wide, :] = qpad_ref[7 + tile_q * k : 9 + tile_q * (k + 1), :]
    for s in range(n_ka):
        q_outs[s][...] = stage_ref[s, 0 : q_outs[s].shape[0], :].astype(BF16)

    offsets = [0]
    for level in range(LEVELS):
        offsets.append(offsets[-1] + (key_rows >> level) * (width >> level))
    finer = None
    for level in reversed(range(LEVELS)):
        w = width >> level
        here = []
        for r in range(key_rows >> level):
            start = offsets[level] + r * w
            value = coarse_ref[start : start + w, :] * (scale * 4.0**-level)
            if finer is not None:
                value = value + finer[r // 2]
            here.append(value)
        if level:
            finer = []
            for value in here:
                put(tmp_ref, pl.ds(0, w, stride=2), value)
                put(tmp_ref, pl.ds(1, w, stride=2), value)
                finer.append(get(tmp_ref, slice(0, 2 * w)))
    for r in range(key_rows):
        put(kpad_ref, pl.ds(key_rows + r, width, stride=key_rows), here[r])
    size = (tile_k + 2) * key_rows
    for s in range(n_quad):
        first = (quad ^ s) * 2 * tile_k * key_rows
        mine = pl.multiple_of(first + core * tile_k * key_rows, 8)
        other = pl.multiple_of(first + (1 - core) * tile_k * key_rows, 8)
        keep_ref[s] = get(kpad_ref, pl.ds(mine, size))
        send_ref[s * size : (s + 1) * size, :] = get(kpad_ref, pl.ds(other, size)).astype(BF16)


def correlate(grads, queries, keys, query_image, key_image, width, key_rows, n_ka, n_quad):
    cells, count = grads.shape
    channels = queries.shape[1]
    rows = count // width
    tile_q = width // n_ka
    tile_k = width // (2 * n_quad)
    size = (tile_k + 2) * key_rows
    counts = [rows * (tile_q + 2) + (tile_k if s and joins(s) else 0) for s in range(n_ka)]
    chunk = 256
    hbm = pl.BlockSpec(memory_space=pltpu.HBM)
    vmem = pl.BlockSpec(memory_space=pltpu.VMEM)
    dims = (width, key_rows, tile_q, tile_k, n_ka, n_quad, chunk)
    lanes = channels // 128
    return pl.pallas_call(
        functools.partial(corr_kernel, dims),
        in_specs=[hbm] * 5,
        out_specs=[vmem] * (n_ka + 2),
        out_shape=[
            jax.ShapeDtypeStruct((count, channels), BF16) for count in counts
        ]
        + [
            jax.ShapeDtypeStruct((n_quad * size + 2 * up16(tile_q), channels), BF16),
            jax.ShapeDtypeStruct((n_quad, size, channels), F32),
        ],
        scratch_shapes=[
            pltpu.VMEM((cells, count), BF16),
            pltpu.VMEM((count, channels), BF16),
            pltpu.VMEM((width * key_rows, channels), BF16),
            pltpu.VMEM((cells, channels), F32),
            pltpu.VMEM((cells, channels), F32),
            pltpu.VMEM((lanes, width * key_rows, 128), F32),
            pltpu.VMEM((lanes, width, 128), F32),
            pltpu.VMEM((lanes, (width + 2) * key_rows, 128), F32),
            pltpu.VMEM((width + 16, channels), F32),
            pltpu.VMEM((n_ka, up16(max(counts)), channels), F32),
            pltpu.VMEM(query_image.shape, BF16),
            pltpu.VMEM(key_image.shape, BF16),
            pltpu.SemaphoreType.DMA((count // chunk + 4,)),
        ],
        compiler_params=pltpu.CompilerParams(vmem_limit_bytes=cells * (count * 4 + channels * 24)),
        name="correlate",
    )(*[pltpu.with_memory_space_constraint(x, pltpu.HBM) for x in (grads, queries, keys, query_image, key_image)])


def pair_kernel(size, tile, keep_ref, recv_ref, own_ref, near_ref, *sends):
    quad, core, _ = place()
    n_quad = len(sends) + 1
    base = n_quad * size
    first = recv_ref[base : base + tile, :].astype(F32)
    last = recv_ref[base + up16(tile) : base + up16(tile) + tile, :].astype(F32)
    near_ref[...] = jnp.where(core == 0, first, last).astype(BF16)
    onward = jnp.where(core == 0, last, first).astype(BF16)
    own_ref[...] = keep_ref[0] + recv_ref[0:size, :].astype(F32)
    for s, send in enumerate(sends, 1):
        send[0:size, :] = (keep_ref[s] + recv_ref[s * size : (s + 1) * size, :].astype(F32)).astype(BF16)
        if joins(s):
            send[size : size + tile, :] = onward


def both_sides(refs, near_ref, size, quad, core):
    tile = near_ref.shape[0]
    parts = [(s, ref[size : size + tile, :].astype(F32)) for s, ref in enumerate(refs, 1) if joins(s)]
    near = near_ref[...].astype(F32)
    far = carried(parts, quad, 2 * core - 1)
    return jnp.where(core == 0, far, near), jnp.where(core == 0, near, far)


def weight_kernel(n_ka, n_quad, *refs):
    q_refs = refs[:n_ka]
    k_refs = refs[n_ka : n_ka + n_quad]
    near_ref, qi_ref, ki_ref = refs[n_ka + n_quad : n_ka + n_quad + 3]
    send_ref, late_ref, keep_ref, gq_ref, gk_ref, acc_ref, sum_ref, ext_ref = refs[n_ka + n_quad + 3 :]
    size, channels = gk_ref.shape
    tile_k, key_rows, cin = ki_ref.shape
    rows, tile_q, _ = qi_ref.shape
    wide = tile_q + 2
    quad, core, z = place()
    top, bottom = both_sides(k_refs[1:], near_ref, size, quad, core)
    lines = [(s, ref[rows * wide : rows * wide + tile_k, :].astype(F32)) for s, ref in enumerate(q_refs) if s and joins(s)]
    ext_ref[:, 8 : 8 + key_rows, :] = ki_ref[...].astype(F32)
    ext_ref[:, 7, :] = carried(lines, z, -1)
    ext_ref[:, 8 + key_rows, :] = carried(lines, z, 1)
    query = jnp.concatenate([top[None], qi_ref[...].astype(F32), bottom[None]], axis=0)
    image = []
    for a in (-1, 0, 1):
        first = query[1 + a : 1 + a + rows].reshape(rows * tile_q, cin)
        second = ext_ref[:, 8 + a : 8 + a + key_rows, :].reshape(tile_k * key_rows, cin)
        image.append(jnp.concatenate([first, second], axis=0).T.astype(BF16))
    image = jnp.concatenate(image, axis=0)
    query = q_refs[0][...].astype(F32)
    for ref in q_refs[1:]:
        query = query + ref[0 : rows * wide, :].astype(F32)
    gq = query.astype(BF16)
    gq_ref[...] = gq
    sum_ref[...] = gq.astype(F32)
    key = k_refs[0][...]
    for ref in k_refs[1:]:
        key = key + ref[0:size, :].astype(F32)
    gk = key.astype(BF16)
    gk_ref[...] = gk
    count = tile_k * key_rows
    for b in (-1, 0, 1):
        starts = [row * wide + 1 - b for row in range(rows)]
        first = jnp.concatenate([sum_ref[start : start + tile_q, :] for start in starts], axis=0).astype(BF16)
        grad = jnp.concatenate([first, gk[(1 - b) * key_rows : (1 - b) * key_rows + count]], axis=0)
        part = jnp.dot(image, grad, preferred_element_type=F32)
        for a in range(3):
            tap = a * 3 + b + 1
            acc_ref[tap * cin : (tap + 1) * cin, :] = part[a * cin : (a + 1) * cin]
    quarter = acc_ref.shape[0] // (2 * n_quad)
    half = n_quad * quarter
    for s in range(n_quad):
        mine = pl.multiple_of(core * half + (quad ^ s) * quarter, 16)
        other = pl.multiple_of((1 - core) * half + (quad ^ s) * quarter, 16)
        keep_ref[s * quarter : (s + 1) * quarter, :] = acc_ref[pl.ds(mine, quarter), :]
        if s:
            send_ref[(s - 1) * quarter : s * quarter, :] = acc_ref[pl.ds(other, quarter), :].astype(BF16)
        else:
            late_ref[0:quarter, :] = acc_ref[pl.ds(other, quarter), :].astype(BF16)
    late_ref[quarter : quarter + wide, :] = sum_ref[0:wide, :].astype(BF16)
    late_ref[quarter + up16(wide) : quarter + up16(wide) + wide, :] = sum_ref[(rows - 1) * wide : rows * wide, :].astype(BF16)


def piece_kernel(keep_ref, recv_ref, *sends):
    size = sends[0].shape[0]
    for s, send in enumerate(sends, 1):
        send[...] = (keep_ref[s * size : (s + 1) * size, :] + recv_ref[(s - 1) * size : s * size, :].astype(F32)).astype(BF16)


def line_kernel(size, late_ref, near_ref, onward_ref):
    _, core, _ = place()
    tile = near_ref.shape[0]
    first = late_ref[size : size + tile, :].astype(F32)
    last = late_ref[size + up16(tile) : size + up16(tile) + tile, :].astype(F32)
    near_ref[...] = jnp.where(core == 0, first, last).astype(BF16)
    onward_ref[...] = jnp.where(core == 0, last, first).astype(BF16)


def layer_kernel(n_quad, *refs):
    keep_ref, *got = refs[: n_quad + 1]
    out_ref, *sends, stage_ref = refs[n_quad + 2 :]
    _, _, z = place()
    n_ka = len(sends) + 1
    size = got[1].shape[0]
    piece = size // n_ka
    total = keep_ref[0:size, :]
    for ref in got:
        total = total + ref[0:size, :].astype(F32)
    for k in range(n_ka):
        stage_ref[z ^ k, 0:piece, :] = total[k * piece : (k + 1) * piece]
    out_ref[...] = stage_ref[0, 0:piece, :]
    for s, send in enumerate(reversed(sends), 1):
        send[...] = stage_ref[s, 0:piece, :].astype(BF16)


def combine_kernel(n_ka, *refs):
    own_ref, *got = refs[:n_ka]
    gk_ref, out_ref, *sends, ext_ref = refs[n_ka:]
    _, _, z = place()
    piece = own_ref.shape[0]
    total = own_ref[...]
    for ref in got:
        total = total + ref[...].astype(F32)
    total = total.astype(BF16)
    out_ref[...] = total
    tall, key_rows, _ = ext_ref.shape
    ext_ref[...] = gk_ref[...].astype(F32).reshape(ext_ref.shape)
    first, last = ext_ref[:, 0, :], ext_ref[:, key_rows - 1, :]
    for s, send in enumerate(reversed(sends), 1):
        send[0:piece, :] = total
        send[piece : piece + tall, :] = jnp.where((z ^ s) == z + 1, last, first).astype(BF16)


def image_kernel(piece, rows, gq_ref, near_ref, far_ref, gk_ref, w_ref, *rest):
    *got, qo_ref, ko_ref, end_ref, qext_ref, kext_ref = rest
    wide, channels = near_ref.shape
    tall = kext_ref.shape[0]
    key_rows = gk_ref.shape[0] // tall
    tile_q = wide - 2
    tile_k = tall - 2
    _, core, z = place()
    near, far = near_ref[...].astype(F32), far_ref[...].astype(F32)
    lines = [(s, ref[piece : piece + tall, :].astype(F32)) for s, ref in enumerate(reversed(got), 1) if joins(s)]
    qext_ref[0, 0:wide, :] = jnp.where(core == 0, far, near)
    query = gq_ref[...].astype(F32)
    for row in range(rows):
        qext_ref[row + 1, 0:wide, :] = query[row * wide : (row + 1) * wide]
    qext_ref[rows + 1, 0:wide, :] = jnp.where(core == 0, near, far)
    kext_ref[:, 8 : 8 + key_rows, :] = gk_ref[...].astype(F32).reshape(tall, key_rows, channels)
    kext_ref[:, 7, :] = carried(lines, z, -1)
    kext_ref[:, 8 + key_rows, :] = carried(lines, z, 1)
    total = None
    for tap in range(9):
        a, b = tap // 3 - 1, tap % 3 - 1
        first = qext_ref[1 - a : 1 - a + rows, 1 - b : 1 - b + tile_q, :].reshape(rows * tile_q, channels)
        second = kext_ref[1 - b : 1 - b + tile_k, 8 - a : 8 - a + key_rows, :].reshape(tile_k * key_rows, channels)
        grad = jnp.concatenate([first.astype(BF16), second.astype(BF16)], axis=0)
        part = lax.dot_general(grad, w_ref[tap], (((1,), (1,)), ((), ())), preferred_element_type=F32)
        total = part if total is None else total + part
    count = qo_ref.shape[0]
    qo_ref[...] = total[:count].astype(BF16)
    ko_ref[...] = total[count:].astype(BF16)
    end_ref[...] = jnp.zeros_like(end_ref)


def gather_kernel(count, axis, *refs):
    own = place()[axis]
    *_, out_ref, stage_ref = refs
    piece = refs[0].shape[0]
    for i in range(count):
        stage_ref[own ^ ((count - i) % count), 0:piece, :] = refs[i][0:piece, :].astype(F32)
    for k in range(count):
        out_ref[k * piece : (k + 1) * piece, :] = stage_ref[k, 0:piece, :].astype(BF16)


def widen_kernel(other, *refs):
    half_ref, out_hbm, wide_ref, sems = refs[0], *refs[-3:]
    _, core, _ = place()
    half = half_ref.shape[0]
    count = sems.shape[0]
    size = half // count
    base = (1 - core if other else core) * half
    copies = []
    for i in range(count):
        wide_ref[i * size : (i + 1) * size, :] = half_ref[i * size : (i + 1) * size, :].astype(F32)
        rows = pl.ds(pl.multiple_of(base + i * size, 8), size)
        copies.append(pltpu.make_async_copy(wide_ref.at[pl.ds(i * size, size)], out_hbm.at[rows], sems.at[i]))
        copies[-1].start()
    for copy in copies:
        copy.wait()


def widen(half, whole=None):
    rows, channels = half.shape
    hbm = pl.BlockSpec(memory_space=pltpu.HBM)
    vmem = pl.BlockSpec(memory_space=pltpu.VMEM)
    more = [] if whole is None else [pltpu.with_memory_space_constraint(whole, pltpu.HBM)]
    return pl.pallas_call(
        functools.partial(widen_kernel, whole is not None),
        in_specs=[vmem] + [hbm] * len(more),
        out_specs=hbm,
        out_shape=jax.ShapeDtypeStruct((2 * rows, channels), F32),
        scratch_shapes=[pltpu.VMEM((rows, channels), F32), pltpu.SemaphoreType.DMA((8,))],
        input_output_aliases={1: 0} if more else {},
        compiler_params=pltpu.CompilerParams(vmem_limit_bytes=SMALL_BYTES),
        name="widen",
    )(half, *more)


def call(kernel, name, outs, args, scratch=(), after=()):
    return pl.pallas_call(
        kernel,
        in_specs=[pl.BlockSpec(memory_space=pltpu.VMEM)] * len(args) + [pl.BlockSpec(memory_space=pl.ANY)] * len(after),
        out_shape=[jax.ShapeDtypeStruct(shape, dtype) for shape, dtype in outs],
        scratch_shapes=[pltpu.VMEM(shape, F32) for shape in scratch],
        compiler_params=pltpu.CompilerParams(vmem_limit_bytes=SMALL_BYTES),
        name=name,
    )(*args, *after)


def body(query_features, key_features, pyramid_grad, query_image, key_image, conv_weight):
    n_pb = lax.axis_size("pb")
    n_ka = lax.axis_size("ka")
    n_quad = n_pb // 2
    quad, core, z = place()
    strip_rows, width, channels = query_features.shape
    key_rows = key_features.shape[1]
    cin = conv_weight.shape[2]
    tile_q = width // n_ka
    tile_k = width // n_pb
    wide = tile_q + 2
    tall = tile_k + 2
    size = tall * key_rows
    taps = 9
    half = taps * cin // 2
    quarter = half // n_quad
    piece = quarter // n_ka

    def to_core(x):
        return lax.ppermute(x, "pb", flip(n_pb, 1))

    def to_quad(parts):
        return [lax.ppermute(x, "pb", flip(n_pb, 2 * s)) for s, x in enumerate(parts, 1)]

    def to_layers(parts):
        return [lax.ppermute(x, "ka", flip(n_ka, s)) for s, x in enumerate(parts, 1)]

    def to_far_layers(parts):
        return [lax.ppermute(x, "ka", flip(n_ka, n_ka - i)) for i, x in enumerate(parts, 1)]

    def extra(count, mask, more):
        return count + (more if joins(mask) else 0)

    grads = jnp.transpose(pyramid_grad.reshape(pyramid_grad.shape[0], pyramid_grad.shape[2]))
    *q_parts, k_send, k_keep = correlate(
        grads,
        query_features.reshape(strip_rows * width, channels),
        key_features.reshape(width * key_rows, channels),
        query_image,
        key_image,
        width,
        key_rows,
        n_ka,
        n_quad,
    )
    k_recv = to_core(k_send)
    q_recv = to_layers(q_parts[1:])
    outs = [((size, channels), F32), ((tile_q, cin), BF16)]
    outs += [((extra(size, s, tile_q), channels), BF16) for s in range(1, n_quad)]
    k_own, near, *k_pair = call(functools.partial(pair_kernel, size, tile_q), "pairs", outs, (k_keep, k_recv))
    k_more = to_quad(k_pair)
    outs = [
        ((half - quarter, channels), BF16),
        ((quarter + 2 * up16(wide), channels), BF16),
        ((half, channels), F32),
        ((strip_rows * wide, channels), BF16),
        ((size, channels), BF16),
    ]
    w_send, w_late, w_keep, gq, gk = call(
        functools.partial(weight_kernel, n_ka, n_quad),
        "weights",
        outs,
        (q_parts[0], *q_recv, k_own, *k_more, near, query_image, key_image),
        [(taps * cin, channels), (strip_rows * wide, channels), (tile_k, key_rows + 16, cin)],
    )

    w_recv = to_core(w_send)
    w_late = to_core(w_late)
    sends = call(piece_kernel, "pieces", [((quarter, channels), BF16)] * (n_quad - 1), (w_keep, w_recv))
    near, far = call(functools.partial(line_kernel, quarter), "lines", [((wide, channels), BF16)] * 2, (w_late,))
    got = to_quad(sends)
    firsts = range(0, n_pb - 2, 2)
    far = lax.ppermute(far, "pb", [(i, i + 2) for i in firsts] + [(i + 3, i + 1) for i in firsts])
    own, *sends = call(
        functools.partial(layer_kernel, n_quad),
        "layers",
        [((piece, channels), F32)] + [((piece, channels), BF16)] * (n_ka - 1),
        (w_keep, w_late, *got),
        [(n_ka, up16(piece), channels)],
        after=(far,),
    )
    got = to_far_layers(sends)
    part, *sends = call(
        functools.partial(combine_kernel, n_ka),
        "combine",
        [((piece, channels), BF16)] + [((piece + tall, channels), BF16)] * (n_ka - 1),
        (own, *got, gk),
        [(tall, key_rows, channels)],
    )
    got = to_far_layers(sends)
    (part,) = call(
        functools.partial(gather_kernel, n_ka, 2),
        "gather",
        [((quarter, channels), BF16)],
        (part, *got),
        [(n_ka, up16(piece), channels)],
    )
    q_out, k_out, end = call(
        functools.partial(image_kernel, piece, strip_rows),
        "images",
        [((strip_rows * tile_q, cin), BF16), ((tile_k * key_rows, cin), BF16), ((8, 128), F32)],
        (gq, near, far, gk, conv_weight.reshape(taps, cin, channels), *got),
        [(strip_rows + 2, up16(wide), channels), (tall, key_rows + 16, channels)],
    )
    (part,) = call(
        functools.partial(gather_kernel, n_quad, 0),
        "gather",
        [((half, channels), BF16)],
        (part, *reversed(to_quad([part] * (n_quad - 1)))),
        [(n_quad, up16(quarter), channels)],
        after=(end,),
    )
    weight_grad = widen(to_core(part), widen(part))
    return (
        q_out.reshape(query_image.shape),
        k_out.reshape(key_image.shape),
        weight_grad.reshape(conv_weight.shape),
    )


def solution(mesh):
    placed = (
        P("pb", None, None),
        P(None, "ka", None),
        P("pb", "ka", None),
        P("pb", "ka", None),
        P("pb", "ka", None),
        P(),
    )
    return jax.shard_map(
        body,
        mesh=mesh,
        in_specs=placed,
        out_specs=(P("pb", "ka", None), P("pb", "ka", None), P()),
        check_vma=False,
    )
```

```python
import functools

import jax
import jax.numpy as jnp
from jax import lax
from jax.experimental import pallas as pl
from jax.experimental.pallas import tpu as pltpu
from jax.sharding import PartitionSpec as P

LEVELS = 4
F32 = jnp.float32
BF16 = jnp.bfloat16
SMALL_BYTES = 16 * 2**20


def flip(count, mask):
    return [(i, i ^ mask) for i in range(count)]


def put(ref, rows, value):
    for lane in range(ref.shape[0]):
        ref[lane, rows, :] = value[:, lane * 128 : (lane + 1) * 128]


def get(ref, rows):
    return jnp.concatenate([ref[lane, rows, :] for lane in range(ref.shape[0])], axis=1)


def up16(count):
    return -(-count // 16) * 16


def joins(mask):
    return (mask & (mask + 1)) == 0


def place():
    pb = lax.axis_index("pb")
    return pb // 2, pb % 2, lax.axis_index("ka")


def carried(parts, index, step):
    total = None
    for mask, row in parts:
        row = jnp.where((index ^ mask) == index + step, row, 0.0)
        total = row if total is None else total + row
    return total


def corr_kernel(dims, a_hbm, q_hbm, key_hbm, qi_hbm, ki_hbm, *rest):
    width, key_rows, tile_q, tile_k, n_ka, n_quad, chunk = dims
    q_outs = rest[:n_ka]
    send_ref, keep_ref = rest[n_ka : n_ka + 2]
    a_ref, q_ref, key_ref, cells_ref, coarse_ref, keyf_ref, tmp_ref, kpad_ref, qpad_ref, stage_ref, qi_ref, ki_ref, sems = rest[n_ka + 2 :]
    count, channels = q_ref.shape
    rows = count // width
    scale = channels ** (-0.5)
    quad, core, z = place()

    copies = [pltpu.make_async_copy(key_hbm, key_ref, sems.at[0])]
    for i in range(count // chunk):
        lanes = pl.ds(i * chunk, chunk)
        copies.append(pltpu.make_async_copy(a_hbm.at[:, lanes], a_ref.at[:, lanes], sems.at[i + 2]))
    copies.append(pltpu.make_async_copy(q_hbm, q_ref, sems.at[1]))
    copies.append(pltpu.make_async_copy(qi_hbm, qi_ref, sems.at[count // chunk + 2]))
    copies.append(pltpu.make_async_copy(ki_hbm, ki_ref, sems.at[count // chunk + 3]))
    for copy in copies:
        copy.start()

    qpad_ref[...] = jnp.zeros_like(qpad_ref)
    edge = jnp.zeros((key_rows, channels), F32)
    put(kpad_ref, slice(0, key_rows), edge)
    put(kpad_ref, slice((width + 1) * key_rows, (width + 2) * key_rows), edge)

    copies[0].wait()
    put(keyf_ref, slice(None), key_ref[...].astype(F32))
    lines = [get(keyf_ref, pl.ds(r, width, stride=key_rows)) for r in range(key_rows)]
    offset = 0
    for level in range(LEVELS):
        w = width >> level
        if level:
            pairs = []
            for i in range(len(lines) // 2):
                put(tmp_ref, slice(0, 2 * w), lines[2 * i] + lines[2 * i + 1])
                pairs.append(get(tmp_ref, pl.ds(0, w, stride=2)) + get(tmp_ref, pl.ds(1, w, stride=2)))
            lines = pairs
        for line in lines:
            cells_ref[offset : offset + w, :] = line * (4.0**-level)
            offset += w
    cells = cells_ref[...].astype(BF16)
    for copy in copies[1:]:
        copy.wait()
    query = lax.dot_general(cells, a_ref[...], (((0,), (0,)), ((), ())), preferred_element_type=F32).T * scale

    last_row = ki_ref[...].astype(F32)
    first_row, last_row = last_row[:, 0], last_row[:, key_rows - 1]
    wide = tile_q + 2
    for s in range(1, n_ka):
        if joins(s):
            stage_ref[s, rows * wide : rows * wide + tile_k, :] = jnp.where((z ^ s) == z + 1, last_row, first_row)
    base = n_quad * (tile_k + 2) * key_rows
    send_ref[base : base + tile_q, :] = qi_ref[0]
    send_ref[base + up16(tile_q) : base + up16(tile_q) + tile_q, :] = qi_ref[rows - 1]
    coarse_ref[...] = jnp.dot(a_ref[...], q_ref[...], preferred_element_type=F32)
    for row in range(rows):
        qpad_ref[8 : 8 + width, :] = query[row * width : (row + 1) * width]
        for k in range(n_ka):
            stage_ref[z ^ k, row * wide : (row + 1) * wide, :] = qpad_ref[7 + tile_q * k : 9 + tile_q * (k + 1), :]
    for s in range(n_ka):
        q_outs[s][...] = stage_ref[s, 0 : q_outs[s].shape[0], :].astype(BF16)

    offsets = [0]
    for level in range(LEVELS):
        offsets.append(offsets[-1] + (key_rows >> level) * (width >> level))
    finer = None
    for level in reversed(range(LEVELS)):
        w = width >> level
        here = []
        for r in range(key_rows >> level):
            start = offsets[level] + r * w
            value = coarse_ref[start : start + w, :] * (scale * 4.0**-level)
            if finer is not None:
                value = value + finer[r // 2]
            here.append(value)
        if level:
            finer = []
            for value in here:
                put(tmp_ref, pl.ds(0, w, stride=2), value)
                put(tmp_ref, pl.ds(1, w, stride=2), value)
                finer.append(get(tmp_ref, slice(0, 2 * w)))
    for r in range(key_rows):
        put(kpad_ref, pl.ds(key_rows + r, width, stride=key_rows), here[r])
    size = (tile_k + 2) * key_rows
    for s in range(n_quad):
        first = (quad ^ s) * 2 * tile_k * key_rows
        mine = pl.multiple_of(first + core * tile_k * key_rows, 8)
        other = pl.multiple_of(first + (1 - core) * tile_k * key_rows, 8)
        keep_ref[s] = get(kpad_ref, pl.ds(mine, size))
        send_ref[s * size : (s + 1) * size, :] = get(kpad_ref, pl.ds(other, size)).astype(BF16)


def correlate(grads, queries, keys, query_image, key_image, width, key_rows, n_ka, n_quad):
    cells, count = grads.shape
    channels = queries.shape[1]
    rows = count // width
    tile_q = width // n_ka
    tile_k = width // (2 * n_quad)
    size = (tile_k + 2) * key_rows
    counts = [rows * (tile_q + 2) + (tile_k if s and joins(s) else 0) for s in range(n_ka)]
    chunk = 256
    hbm = pl.BlockSpec(memory_space=pltpu.HBM)
    vmem = pl.BlockSpec(memory_space=pltpu.VMEM)
    dims = (width, key_rows, tile_q, tile_k, n_ka, n_quad, chunk)
    lanes = channels // 128
    return pl.pallas_call(
        functools.partial(corr_kernel, dims),
        in_specs=[hbm] * 5,
        out_specs=[vmem] * (n_ka + 2),
        out_shape=[
            jax.ShapeDtypeStruct((count, channels), BF16) for count in counts
        ]
        + [
            jax.ShapeDtypeStruct((n_quad * size + 2 * up16(tile_q), channels), BF16),
            jax.ShapeDtypeStruct((n_quad, size, channels), F32),
        ],
        scratch_shapes=[
            pltpu.VMEM((cells, count), BF16),
            pltpu.VMEM((count, channels), BF16),
            pltpu.VMEM((width * key_rows, channels), BF16),
            pltpu.VMEM((cells, channels), F32),
            pltpu.VMEM((cells, channels), F32),
            pltpu.VMEM((lanes, width * key_rows, 128), F32),
            pltpu.VMEM((lanes, width, 128), F32),
            pltpu.VMEM((lanes, (width + 2) * key_rows, 128), F32),
            pltpu.VMEM((width + 16, channels), F32),
            pltpu.VMEM((n_ka, up16(max(counts)), channels), F32),
            pltpu.VMEM(query_image.shape, BF16),
            pltpu.VMEM(key_image.shape, BF16),
            pltpu.SemaphoreType.DMA((count // chunk + 4,)),
        ],
        compiler_params=pltpu.CompilerParams(vmem_limit_bytes=cells * (count * 4 + channels * 24)),
        name="correlate",
    )(*[pltpu.with_memory_space_constraint(x, pltpu.HBM) for x in (grads, queries, keys, query_image, key_image)])


def pair_kernel(size, tile, keep_ref, recv_ref, own_ref, near_ref, *sends):
    quad, core, _ = place()
    n_quad = len(sends) + 1
    base = n_quad * size
    first = recv_ref[base : base + tile, :].astype(F32)
    last = recv_ref[base + up16(tile) : base + up16(tile) + tile, :].astype(F32)
    near_ref[...] = jnp.where(core == 0, first, last).astype(BF16)
    onward = jnp.where(core == 0, last, first).astype(BF16)
    own_ref[...] = keep_ref[0] + recv_ref[0:size, :].astype(F32)
    for s, send in enumerate(sends, 1):
        send[0:size, :] = (keep_ref[s] + recv_ref[s * size : (s + 1) * size, :].astype(F32)).astype(BF16)
        if joins(s):
            send[size : size + tile, :] = onward


def both_sides(refs, near_ref, size, quad, core):
    tile = near_ref.shape[0]
    parts = [(s, ref[size : size + tile, :].astype(F32)) for s, ref in enumerate(refs, 1) if joins(s)]
    near = near_ref[...].astype(F32)
    far = carried(parts, quad, 2 * core - 1)
    return jnp.where(core == 0, far, near), jnp.where(core == 0, near, far)


def weight_kernel(n_ka, n_quad, *refs):
    q_refs = refs[:n_ka]
    k_refs = refs[n_ka : n_ka + n_quad]
    near_ref, qi_ref, ki_ref = refs[n_ka + n_quad : n_ka + n_quad + 3]
    send_ref, late_ref, keep_ref, gq_ref, gk_ref, acc_ref, sum_ref, ext_ref = refs[n_ka + n_quad + 3 :]
    size, channels = gk_ref.shape
    tile_k, key_rows, cin = ki_ref.shape
    rows, tile_q, _ = qi_ref.shape
    wide = tile_q + 2
    quad, core, z = place()
    top, bottom = both_sides(k_refs[1:], near_ref, size, quad, core)
    lines = [(s, ref[rows * wide : rows * wide + tile_k, :].astype(F32)) for s, ref in enumerate(q_refs) if s and joins(s)]
    ext_ref[:, 8 : 8 + key_rows, :] = ki_ref[...].astype(F32)
    ext_ref[:, 7, :] = carried(lines, z, -1)
    ext_ref[:, 8 + key_rows, :] = carried(lines, z, 1)
    query = jnp.concatenate([top[None], qi_ref[...].astype(F32), bottom[None]], axis=0)
    image = []
    for a in (-1, 0, 1):
        first = query[1 + a : 1 + a + rows].reshape(rows * tile_q, cin)
        second = ext_ref[:, 8 + a : 8 + a + key_rows, :].reshape(tile_k * key_rows, cin)
        image.append(jnp.concatenate([first, second], axis=0).T.astype(BF16))
    image = jnp.concatenate(image, axis=0)
    query = q_refs[0][...].astype(F32)
    for ref in q_refs[1:]:
        query = query + ref[0 : rows * wide, :].astype(F32)
    gq = query.astype(BF16)
    gq_ref[...] = gq
    sum_ref[...] = gq.astype(F32)
    key = k_refs[0][...]
    for ref in k_refs[1:]:
        key = key + ref[0:size, :].astype(F32)
    gk = key.astype(BF16)
    gk_ref[...] = gk
    count = tile_k * key_rows
    for b in (-1, 0, 1):
        starts = [row * wide + 1 - b for row in range(rows)]
        first = jnp.concatenate([sum_ref[start : start + tile_q, :] for start in starts], axis=0).astype(BF16)
        grad = jnp.concatenate([first, gk[(1 - b) * key_rows : (1 - b) * key_rows + count]], axis=0)
        part = jnp.dot(image, grad, preferred_element_type=F32)
        for a in range(3):
            tap = a * 3 + b + 1
            acc_ref[tap * cin : (tap + 1) * cin, :] = part[a * cin : (a + 1) * cin]
    quarter = acc_ref.shape[0] // (2 * n_quad)
    half = n_quad * quarter
    for s in range(n_quad):
        mine = pl.multiple_of(core * half + (quad ^ s) * quarter, 16)
        other = pl.multiple_of((1 - core) * half + (quad ^ s) * quarter, 16)
        keep_ref[s * quarter : (s + 1) * quarter, :] = acc_ref[pl.ds(mine, quarter), :]
        if s:
            send_ref[(s - 1) * quarter : s * quarter, :] = acc_ref[pl.ds(other, quarter), :].astype(BF16)
        else:
            late_ref[0:quarter, :] = acc_ref[pl.ds(other, quarter), :].astype(BF16)
    late_ref[quarter : quarter + wide, :] = sum_ref[0:wide, :].astype(BF16)
    late_ref[quarter + up16(wide) : quarter + up16(wide) + wide, :] = sum_ref[(rows - 1) * wide : rows * wide, :].astype(BF16)


def piece_kernel(keep_ref, recv_ref, *sends):
    size = sends[0].shape[0]
    for s, send in enumerate(sends, 1):
        send[...] = (keep_ref[s * size : (s + 1) * size, :] + recv_ref[(s - 1) * size : s * size, :].astype(F32)).astype(BF16)


def line_kernel(size, late_ref, near_ref, onward_ref):
    _, core, _ = place()
    tile = near_ref.shape[0]
    first = late_ref[size : size + tile, :].astype(F32)
    last = late_ref[size + up16(tile) : size + up16(tile) + tile, :].astype(F32)
    near_ref[...] = jnp.where(core == 0, first, last).astype(BF16)
    onward_ref[...] = jnp.where(core == 0, last, first).astype(BF16)


def layer_kernel(n_quad, *refs):
    keep_ref, *got = refs[: n_quad + 1]
    out_ref, *sends, stage_ref = refs[n_quad + 2 :]
    _, _, z = place()
    n_ka = len(sends) + 1
    size = got[1].shape[0]
    piece = size // n_ka
    total = keep_ref[0:size, :]
    for ref in got:
        total = total + ref[0:size, :].astype(F32)
    for k in range(n_ka):
        stage_ref[z ^ k, 0:piece, :] = total[k * piece : (k + 1) * piece]
    out_ref[...] = stage_ref[0, 0:piece, :]
    for s, send in enumerate(reversed(sends), 1):
        send[...] = stage_ref[s, 0:piece, :].astype(BF16)


def combine_kernel(n_ka, *refs):
    own_ref, *got = refs[:n_ka]
    gk_ref, out_ref, *sends, ext_ref = refs[n_ka:]
    _, _, z = place()
    piece = own_ref.shape[0]
    total = own_ref[...]
    for ref in got:
        total = total + ref[...].astype(F32)
    total = total.astype(BF16)
    out_ref[...] = total
    tall, key_rows, _ = ext_ref.shape
    ext_ref[...] = gk_ref[...].astype(F32).reshape(ext_ref.shape)
    first, last = ext_ref[:, 0, :], ext_ref[:, key_rows - 1, :]
    for s, send in enumerate(reversed(sends), 1):
        send[0:piece, :] = total
        send[piece : piece + tall, :] = jnp.where((z ^ s) == z + 1, last, first).astype(BF16)


def image_kernel(piece, rows, gq_ref, near_ref, far_ref, gk_ref, w_ref, *rest):
    *got, qo_ref, ko_ref, end_ref, qext_ref, kext_ref = rest
    wide, channels = near_ref.shape
    tall = kext_ref.shape[0]
    key_rows = gk_ref.shape[0] // tall
    tile_q = wide - 2
    tile_k = tall - 2
    _, core, z = place()
    near, far = near_ref[...].astype(F32), far_ref[...].astype(F32)
    lines = [(s, ref[piece : piece + tall, :].astype(F32)) for s, ref in enumerate(reversed(got), 1) if joins(s)]
    qext_ref[0, 0:wide, :] = jnp.where(core == 0, far, near)
    query = gq_ref[...].astype(F32)
    for row in range(rows):
        qext_ref[row + 1, 0:wide, :] = query[row * wide : (row + 1) * wide]
    qext_ref[rows + 1, 0:wide, :] = jnp.where(core == 0, near, far)
    kext_ref[:, 8 : 8 + key_rows, :] = gk_ref[...].astype(F32).reshape(tall, key_rows, channels)
    kext_ref[:, 7, :] = carried(lines, z, -1)
    kext_ref[:, 8 + key_rows, :] = carried(lines, z, 1)
    total = None
    for tap in range(9):
        a, b = tap // 3 - 1, tap % 3 - 1
        first = qext_ref[1 - a : 1 - a + rows, 1 - b : 1 - b + tile_q, :].reshape(rows * tile_q, channels)
        second = kext_ref[1 - b : 1 - b + tile_k, 8 - a : 8 - a + key_rows, :].reshape(tile_k * key_rows, channels)
        grad = jnp.concatenate([first.astype(BF16), second.astype(BF16)], axis=0)
        part = lax.dot_general(grad, w_ref[tap], (((1,), (1,)), ((), ())), preferred_element_type=F32)
        total = part if total is None else total + part
    count = qo_ref.shape[0]
    qo_ref[...] = total[:count].astype(BF16)
    ko_ref[...] = total[count:].astype(BF16)
    end_ref[...] = jnp.zeros_like(end_ref)


def gather_kernel(count, axis, *refs):
    own = place()[axis]
    *_, out_ref, stage_ref = refs
    piece = refs[0].shape[0]
    for i in range(count):
        stage_ref[own ^ ((count - i) % count), 0:piece, :] = refs[i][0:piece, :].astype(F32)
    for k in range(count):
        out_ref[k * piece : (k + 1) * piece, :] = stage_ref[k, 0:piece, :].astype(BF16)


def widen_kernel(other, *refs):
    half_ref, out_hbm, wide_ref, sems = refs[0], *refs[-3:]
    _, core, _ = place()
    half = half_ref.shape[0]
    count = sems.shape[0]
    size = half // count
    base = (1 - core if other else core) * half
    copies = []
    for i in range(count):
        wide_ref[i * size : (i + 1) * size, :] = half_ref[i * size : (i + 1) * size, :].astype(F32)
        rows = pl.ds(pl.multiple_of(base + i * size, 8), size)
        copies.append(pltpu.make_async_copy(wide_ref.at[pl.ds(i * size, size)], out_hbm.at[rows], sems.at[i]))
        copies[-1].start()
    for copy in copies:
        copy.wait()


def widen(half, whole=None):
    rows, channels = half.shape
    hbm = pl.BlockSpec(memory_space=pltpu.HBM)
    vmem = pl.BlockSpec(memory_space=pltpu.VMEM)
    more = [] if whole is None else [pltpu.with_memory_space_constraint(whole, pltpu.HBM)]
    return pl.pallas_call(
        functools.partial(widen_kernel, whole is not None),
        in_specs=[vmem] + [hbm] * len(more),
        out_specs=hbm,
        out_shape=jax.ShapeDtypeStruct((2 * rows, channels), F32),
        scratch_shapes=[pltpu.VMEM((rows, channels), F32), pltpu.SemaphoreType.DMA((3,))],
        input_output_aliases={1: 0} if more else {},
        compiler_params=pltpu.CompilerParams(vmem_limit_bytes=SMALL_BYTES),
        name="widen",
    )(half, *more)


def call(kernel, name, outs, args, scratch=(), after=()):
    return pl.pallas_call(
        kernel,
        in_specs=[pl.BlockSpec(memory_space=pltpu.VMEM)] * len(args) + [pl.BlockSpec(memory_space=pl.ANY)] * len(after),
        out_shape=[jax.ShapeDtypeStruct(shape, dtype) for shape, dtype in outs],
        scratch_shapes=[pltpu.VMEM(shape, F32) for shape in scratch],
        compiler_params=pltpu.CompilerParams(vmem_limit_bytes=SMALL_BYTES),
        name=name,
    )(*args, *after)


def body(query_features, key_features, pyramid_grad, query_image, key_image, conv_weight):
    n_pb = lax.axis_size("pb")
    n_ka = lax.axis_size("ka")
    n_quad = n_pb // 2
    quad, core, z = place()
    strip_rows, width, channels = query_features.shape
    key_rows = key_features.shape[1]
    cin = conv_weight.shape[2]
    tile_q = width // n_ka
    tile_k = width // n_pb
    wide = tile_q + 2
    tall = tile_k + 2
    size = tall * key_rows
    taps = 9
    half = taps * cin // 2
    quarter = half // n_quad
    piece = quarter // n_ka

    def to_core(x):
        return lax.ppermute(x, "pb", flip(n_pb, 1))

    def to_quad(parts):
        return [lax.ppermute(x, "pb", flip(n_pb, 2 * s)) for s, x in enumerate(parts, 1)]

    def to_layers(parts):
        return [lax.ppermute(x, "ka", flip(n_ka, s)) for s, x in enumerate(parts, 1)]

    def to_far_layers(parts):
        return [lax.ppermute(x, "ka", flip(n_ka, n_ka - i)) for i, x in enumerate(parts, 1)]

    def extra(count, mask, more):
        return count + (more if joins(mask) else 0)

    grads = jnp.transpose(pyramid_grad.reshape(pyramid_grad.shape[0], pyramid_grad.shape[2]))
    *q_parts, k_send, k_keep = correlate(
        grads,
        query_features.reshape(strip_rows * width, channels),
        key_features.reshape(width * key_rows, channels),
        query_image,
        key_image,
        width,
        key_rows,
        n_ka,
        n_quad,
    )
    k_recv = to_core(k_send)
    q_recv = to_layers(q_parts[1:])
    outs = [((size, channels), F32), ((tile_q, cin), BF16)]
    outs += [((extra(size, s, tile_q), channels), BF16) for s in range(1, n_quad)]
    k_own, near, *k_pair = call(functools.partial(pair_kernel, size, tile_q), "pairs", outs, (k_keep, k_recv))
    k_more = to_quad(k_pair)
    outs = [
        ((half - quarter, channels), BF16),
        ((quarter + 2 * up16(wide), channels), BF16),
        ((half, channels), F32),
        ((strip_rows * wide, channels), BF16),
        ((size, channels), BF16),
    ]
    w_send, w_late, w_keep, gq, gk = call(
        functools.partial(weight_kernel, n_ka, n_quad),
        "weights",
        outs,
        (q_parts[0], *q_recv, k_own, *k_more, near, query_image, key_image),
        [(taps * cin, channels), (strip_rows * wide, channels), (tile_k, key_rows + 16, cin)],
    )

    w_recv = to_core(w_send)
    w_late = to_core(w_late)
    sends = call(piece_kernel, "pieces", [((quarter, channels), BF16)] * (n_quad - 1), (w_keep, w_recv))
    near, far = call(functools.partial(line_kernel, quarter), "lines", [((wide, channels), BF16)] * 2, (w_late,))
    got = to_quad(sends)
    firsts = range(0, n_pb - 2, 2)
    far = lax.ppermute(far, "pb", [(i, i + 2) for i in firsts] + [(i + 3, i + 1) for i in firsts])
    own, *sends = call(
        functools.partial(layer_kernel, n_quad),
        "layers",
        [((piece, channels), F32)] + [((piece, channels), BF16)] * (n_ka - 1),
        (w_keep, w_late, *got),
        [(n_ka, up16(piece), channels)],
        after=(far,),
    )
    got = to_far_layers(sends)
    part, *sends = call(
        functools.partial(combine_kernel, n_ka),
        "combine",
        [((piece, channels), BF16)] + [((piece + tall, channels), BF16)] * (n_ka - 1),
        (own, *got, gk),
        [(tall, key_rows, channels)],
    )
    got = to_far_layers(sends)
    (part,) = call(
        functools.partial(gather_kernel, n_ka, 2),
        "gather",
        [((quarter, channels), BF16)],
        (part, *got),
        [(n_ka, up16(piece), channels)],
    )
    q_out, k_out, end = call(
        functools.partial(image_kernel, piece, strip_rows),
        "images",
        [((strip_rows * tile_q, cin), BF16), ((tile_k * key_rows, cin), BF16), ((8, 128), F32)],
        (gq, near, far, gk, conv_weight.reshape(taps, cin, channels), *got),
        [(strip_rows + 2, up16(wide), channels), (tall, key_rows + 16, channels)],
    )
    (part,) = call(
        functools.partial(gather_kernel, n_quad, 0),
        "gather",
        [((half, channels), BF16)],
        (part, *reversed(to_quad([part] * (n_quad - 1)))),
        [(n_quad, up16(quarter), channels)],
        after=(end,),
    )
    weight_grad = widen(to_core(part), widen(part))
    return (
        q_out.reshape(query_image.shape),
        k_out.reshape(key_image.shape),
        weight_grad.reshape(conv_weight.shape),
    )


def solution(mesh):
    placed = (
        P("pb", None, None),
        P(None, "ka", None),
        P("pb", "ka", None),
        P("pb", "ka", None),
        P("pb", "ka", None),
        P(),
    )
    return jax.shard_map(
        body,
        mesh=mesh,
        in_specs=placed,
        out_specs=(P("pb", "ka", None), P("pb", "ka", None), P()),
        check_vma=False,
    )
```
